256 devices in a mesh: cluster: 8 (over y, core), sub: 32 (over x, z).
Axes of the slice: x: 4, y: 4, z: 8, core: 2. Of those that a mesh axis runs over, the one named last changes fastest.
Arguments:
- compliance: float32 [8, 32, 1024, 1024], P('cluster', 'sub'), may hold values from -0.078125 to 4.078125, as said below
- loads: float32 [8, 32, 1024, 256], P('cluster', 'sub'), may hold values from -6 to 6
- modes: float32 [8, 32, 32, 1024], P('cluster', 'sub'), may hold values from -1 to 1
- coarse_inverse: float32 [8, 1024, 1024], P('cluster', 'sub'), may hold values from -0.9 to 0.9, as said below
- face_block: int32 [8, 32, 4], replicated, may hold values from 0 to 7, as said below
- edge_rows: int32 [8, 32, 2], replicated, may hold values from 16 to 128
Outputs:
- solution: float32 [8, 32, 1024, 256], P('cluster', 'sub')
- residual: float32 [8, 32, 1024, 256], P('cluster', 'sub')
The draws below stay inside these ranges and needn't reach their ends.
Inputs may be any that keep to these rules, and one draw needn't show every extreme that they name: `compliance`: symmetric positive definite for every subdomain. `coarse_inverse`: symmetric positive definite for every cluster. `face_block`: the four faces of a subdomain lie in four different row blocks. `edge_rows`: entries of faces with no partner are not read.
All inputs are finite; a program needn't handle non-finite values.
Results may differ from the reference program's by a relative error of at most 0.00018.
Values sent between devices are 32-bit elements; how exact they have to be, the bound alone decides.
A program may use at most 64 MiB of HBM per device.

```python
import jax
import jax.numpy as jnp
from jax import lax

ORDER = 1024
BLOCK = 128
MODES = 32
LOADS = 256
ITERS = 3
CMODES = 1024
N_CLUSTER = 8
N_SUB = 32


def draw_compliance(key, part):
    count = N_CLUSTER * N_SUB
    keys = jax.random.split(key, count)

    def single(subkey):
        first, second = jax.random.split(subkey)
        diag = jnp.exp(jax.random.uniform(first, (ORDER,), jnp.float32, jnp.log(2.0), jnp.log(4.0)))
        noise = jnp.clip(jax.random.normal(second, (ORDER, ORDER), jnp.float32), -5.0, 5.0) * (0.5 / ORDER ** 0.5)
        return 0.5 * (noise + noise.T) + jnp.diag(diag)
    return lax.map(single, keys).reshape(N_CLUSTER, N_SUB, ORDER, ORDER)


def draw_coarse_inverse(key, part):
    keys = jax.random.split(jax.random.fold_in(key, 7), N_CLUSTER)

    def single(subkey):
        base = jnp.clip(jax.random.normal(subkey, (CMODES, CMODES), jnp.float32), -4.0, 4.0)
        gram = jnp.dot(base, base.T, precision=lax.Precision.HIGHEST) / CMODES
        return 0.05 * gram + 0.05 * jnp.eye(CMODES, dtype=jnp.float32)
    return lax.map(single, keys)


def draw_face_block(key, part):
    nblocks = ORDER // BLOCK
    scores = jax.random.randint(jax.random.fold_in(key, 11), (N_CLUSTER, N_SUB, nblocks), 0, 1 << 20)
    scores = scores * nblocks + jnp.arange(nblocks, dtype=jnp.int32)
    order = jnp.argsort(scores, axis=-1)
    return order[..., :4].astype(jnp.int32)


def with_ends(entries, key, smallest, largest):
    index_at = [jax.random.randint(jax.random.fold_in(key, axis), (), 0, length) for axis, length in enumerate(entries.shape)]
    main_axis = entries.shape.index(max(entries.shape))
    next_to = index_at[:main_axis] + [(index_at[main_axis] + 1) % entries.shape[main_axis]] + index_at[main_axis + 1:]
    return entries.at[tuple(index_at)].set(smallest).at[tuple(next_to)].set(largest)


def level_of(rng, extent, pieces, least, largest):
    level, own = 1.0, jax.random.fold_in(rng, 6)
    for axis_at, blocks in pieces:
        draws = jnp.exp(jax.random.uniform(jax.random.fold_in(own, axis_at), (blocks,), jnp.float32, least / len(pieces), largest / len(pieces)))
        level = level * jnp.repeat(draws, extent[axis_at] // blocks).reshape([-1 if axis == axis_at else 1 for axis in range(len(extent))])
    return level


def scatter_about(own_key, dims, scale, bound, cuts=(), kind=jnp.bfloat16):
    entries = jax.random.normal(own_key, dims, jnp.float32) * scale
    if len(cuts) > 0:
        entries = level_of(own_key, dims, cuts, -0.22, 0.18) * entries
    return jnp.clip(entries, min=-bound, max=bound).astype(kind)


def setup_inputs(seed: int = 0) -> dict:
    splits = jax.random.split(jax.random.key(seed), 7)
    compliance = draw_compliance(jax.random.fold_in(splits[6], 71), 0)
    loads = scatter_about(splits[1], (N_CLUSTER, N_SUB, ORDER, LOADS), 1.0, 6.0, ((0, 8), (1, 32)), jnp.float32)
    modes = scatter_about(splits[2], (N_CLUSTER, N_SUB, MODES, ORDER), MODES ** -0.5, 1.0, ((0, 8), (1, 32)), jnp.float32)
    coarse_inverse = draw_coarse_inverse(jax.random.fold_in(splits[6], 71), 0)
    face_block = draw_face_block(jax.random.fold_in(splits[6], 71), 0)
    edge_rows = with_ends(jax.random.randint(splits[5], (N_CLUSTER, N_SUB, 2), BLOCK // 8, BLOCK + 1), jax.random.fold_in(splits[5], 1), BLOCK // 8, BLOCK).astype(jnp.int32)
    return dict(compliance=compliance, loads=loads, modes=modes, coarse_inverse=coarse_inverse, face_block=face_block, edge_rows=edge_rows)


def face_values(blocks, onehot, face):
    return jnp.einsum('csb,csbrl->csrl', onehot[:, :, face, :], blocks, precision=lax.Precision.HIGHEST)


def assemble(field, face_block, edge_rows):
    nclus, nsub = field.shape[0], field.shape[1]
    nblocks = ORDER // BLOCK
    width = field.shape[-1]
    blocks = field.reshape(nclus, nsub, nblocks, BLOCK, width)
    onehot = (face_block[..., None] == jnp.arange(nblocks, dtype=jnp.int32)).astype(field.dtype)
    rows = jnp.arange(BLOCK, dtype=jnp.int32)
    values = [face_values(blocks, onehot, face) for face in range(4)]
    sub_mask = (rows < edge_rows[:, :-1, 0, None]).astype(field.dtype)[..., None]
    clus_mask = (rows < edge_rows[:-1, :, 1, None]).astype(field.dtype)[..., None]
    zero4 = (0, 0)
    added = [
        jnp.pad(0.5 * sub_mask * values[1][:, :-1], (zero4, (1, 0), zero4, zero4)),
        jnp.pad(0.5 * sub_mask * values[0][:, 1:], (zero4, (0, 1), zero4, zero4)),
        jnp.pad(0.5 * clus_mask * values[3][:-1], ((1, 0), zero4, zero4, zero4)),
        jnp.pad(0.5 * clus_mask * values[2][1:], ((0, 1), zero4, zero4, zero4)),
    ]
    total = jnp.zeros_like(blocks)
    for face in range(4):
        total = total + onehot[:, :, face, :, None, None] * added[face][:, :, None, :, :]
    return field + total.reshape(field.shape)


def local_apply(compliance, field):
    nclus, nsub = field.shape[0], field.shape[1]
    mats = compliance.reshape(nclus * nsub, ORDER, ORDER)
    vecs = field.reshape(nclus * nsub, ORDER, field.shape[-1])
    out = lax.map(lambda pair: jnp.dot(pair[0], pair[1], precision=lax.Precision.HIGHEST), (mats, vecs))
    return out.reshape(field.shape)


def operator(compliance, face_block, edge_rows, field):
    return assemble(local_apply(compliance, assemble(field, face_block, edge_rows)), face_block, edge_rows)


def precondition(modes, coarse_inverse, resid):
    nclus, nsub = resid.shape[0], resid.shape[1]
    coarse = jnp.einsum('csmo,csol->csml', modes, resid, precision=lax.Precision.HIGHEST)
    stacked = coarse.reshape(nclus, nsub * MODES, resid.shape[-1])
    solved = jnp.einsum('cij,cjl->cil', coarse_inverse, stacked, precision=lax.Precision.HIGHEST)
    solved = solved.reshape(nclus, nsub, MODES, resid.shape[-1])
    return resid + jnp.einsum('csmo,csml->csol', modes, solved, precision=lax.Precision.HIGHEST)


def column_sums(left, right):
    return jnp.sum(left * right, axis=(0, 1, 2))


def reference(compliance, loads, modes, coarse_inverse, face_block, edge_rows):
    solution = jnp.zeros_like(loads)
    residual = loads
    precond = precondition(modes, coarse_inverse, residual)
    direction = precond
    rz_now = column_sums(residual, precond)
    for step in range(ITERS):
        image = operator(compliance, face_block, edge_rows, direction)
        alpha = rz_now / column_sums(direction, image)
        solution = solution + alpha * direction
        residual = residual - alpha * image
        if step + 1 < ITERS:
            precond = precondition(modes, coarse_inverse, residual)
            rz_next = column_sums(residual, precond)
            direction = precond + (rz_next / rz_now) * direction
            rz_now = rz_next
    return solution, residual
```

```python
import functools

import jax
import jax.numpy as jnp
from jax import lax
from jax.experimental import pallas as pl
from jax.experimental.pallas import tpu as pltpu
from jax.sharding import PartitionSpec as P

BLOCK = 128
NBLOCKS = 8
ORDER = BLOCK * NBLOCKS
FACE_ROWS = 4 * BLOCK
MODES = 32
SUMS = 8
PACK = MODES + SUMS
ITERS = 3
NZ = 8
CHUNK = 64
F32 = jnp.float32
BF16 = jnp.bfloat16


def split(value):
    high = value.astype(BF16)
    return high, (value - high.astype(F32)).astype(BF16)


def mm(left, right):
    return jnp.dot(left, right, preferred_element_type=F32)


def same(left, right):
    gap = left - right
    return 1 - jnp.minimum(gap * gap, 1)


def fold(value):
    rows, width = value.shape
    return jnp.sum(value.reshape(rows // 8, 8, width), axis=0)


def remote(src, dst, send_sem, recv_sem, device):
    return pltpu.make_async_remote_copy(
        src_ref=src, dst_ref=dst, send_sem=send_sem, recv_sem=recv_sem,
        device_id=device, device_id_type=pl.DeviceIdType.MESH,
    )


def kernel(nx, nz, nc, comp, loads, modes, cinv, fb, er, x_out, r_out, m):
    ns = nx * nz
    c = lax.axis_index("cluster")
    s = lax.axis_index("sub")
    xm = lax.div(s, nz)
    zm = lax.rem(s, nz)
    width = m.raw.shape[1]

    def z_at(step):
        return lax.rem(zm + (step + nz), nz)

    def x_at(step):
        return lax.rem(xm + (step + nx), nx)

    def c_at(step):
        return lax.rem(c + (step + nc), nc)

    def z_peer(step):
        return (c, xm * nz + z_at(step))

    def x_peer(step):
        return (c, x_at(step) * nz + zm)

    def c_peer(step):
        return (c_at(step), s)

    beside = (
        (c, lax.rem(s + ns - 1, ns)),
        (c, lax.rem(s + 1, ns)),
        (c_at(-1), s),
        (c_at(1), s),
    )

    get_loads = pltpu.make_async_copy(loads.at[0, 0], m.raw, m.lsem.at[0])
    get_modes = pltpu.make_async_copy(modes.at[0, 0], m.braw, m.lsem.at[1])
    get_cinv = pltpu.make_async_copy(cinv.at[0], m.mraw, m.lsem.at[2])
    get_comp = pltpu.make_async_copy(comp.at[0, 0], m.craw, m.lsem.at[3])
    get_fb = pltpu.make_async_copy(fb.at[c], m.fbs, m.lsem.at[4])
    get_er = pltpu.make_async_copy(er.at[c], m.ers.at[0], m.lsem.at[5])
    get_er_low = pltpu.make_async_copy(er.at[jnp.maximum(c - 1, 0)], m.ers.at[1], m.lsem.at[6])
    for copy in (get_fb, get_er, get_er_low, get_loads, get_modes, get_cinv, get_comp):
        copy.start()

    barrier = pltpu.get_barrier_semaphore()
    greeted = (
        [z_peer(step) for step in range(1, nz)]
        + [x_peer(step) for step in range(1, nx)]
        + [c_peer(step) for step in range(1, nc)]
        + [beside[0], beside[1]]
    )
    for peer in greeted:
        pl.semaphore_signal(barrier, inc=1, device_id=peer, device_id_type=pl.DeviceIdType.MESH)

    for copy in (get_fb, get_er, get_er_low):
        copy.wait()
    faces = [m.fbs[s, f] for f in range(4)]
    rank = jnp.int32(0)
    pick = [[] for _ in range(NBLOCKS)]
    for b in range(NBLOCKS):
        hits = [same(face, b) for face in faces]
        free = 1 - (hits[0] + hits[1] + hits[2] + hits[3])
        hits = hits + [free * same(rank, j) for j in range(4)]
        for p in range(NBLOCKS):
            pick[p].append(hits[p].astype(F32))
        rank = rank + free

    def gathered(p, parts):
        value = pick[p][0] * parts[0]
        for b in range(1, NBLOCKS):
            value = value + pick[p][b] * parts[b]
        return value

    def scattered(b, parts):
        value = pick[0][b] * parts[0]
        for p in range(1, NBLOCKS):
            value = value + pick[p][b] * parts[p]
        return value

    shared = [
        m.ers[0, jnp.maximum(s - 1, 0), 0] * jnp.minimum(s, 1),
        m.ers[0, s, 0] * jnp.minimum(ns - 1 - s, 1),
        m.ers[1, s, 1] * jnp.minimum(c, 1),
        m.ers[0, s, 1] * jnp.minimum(nc - 1 - c, 1),
    ]
    row_at = lax.broadcasted_iota(jnp.int32, (BLOCK, width), 0)
    for f in range(4):
        m.weight[pl.ds(f * BLOCK, BLOCK), :] = 0.5 * jnp.clip(shared[f] - row_at, 0, 1).astype(F32)

    def halved(face, value):
        return m.weight[pl.ds(face * BLOCK, BLOCK), :] * value

    def rows(p):
        return pl.ds(p * BLOCK, BLOCK)

    def loop_rows(first, count, body):
        def step(i, carry):
            body(pl.ds(pl.multiple_of(first + i * CHUNK, CHUNK), CHUNK))
            return carry
        lax.fori_loop(0, count // CHUNK, step, 0)

    def to_halves(source):
        def body(at):
            high, low = split(source[at, :])
            m.vhi[at, :] = high
            m.vlo[at, :] = low
        return body

    get_modes.wait()
    high, low = split(m.braw[...])
    m.bhl[0:MODES, :] = high
    m.bhl[MODES:2 * MODES, :] = low
    get_loads.wait()
    loop_rows(0, ORDER, to_halves(m.raw))

    def coarse(first, count):
        ks = pl.ds(first, count)
        both = mm(m.bhl[:, ks], m.vhi[ks, :])
        return both[:MODES] + both[MODES:] + mm(m.bhl[0:MODES, ks], m.vlo[ks, :])

    pending = []

    def send(src, dst, send_sem, recv_sem, device):
        copy = remote(src, dst, send_sem, recv_sem, device)
        copy.start()
        pending.append(copy)

    far_first = sorted(range(1, nz), key=lambda step: -min(step, nz - step))

    def z_gather_start(k):
        for step in far_first:
            mine = m.zg.at[k, zm]
            send(mine, mine, m.zss.at[k, step], m.zrs.at[k, step], z_peer(step))

    def z_gather_wait(k):
        for step in reversed(far_first):
            slot = m.zg.at[k, z_at(-step)]
            remote(slot, slot, m.zss.at[k, step], m.zrs.at[k, step], z_peer(step)).wait_recv()

    m.zg[0, zm, 0:MODES, :] = coarse(0, ORDER)
    m.zg[0, zm, MODES:PACK, :] = jnp.zeros((SUMS, width), F32)
    pl.semaphore_wait(barrier, len(greeted))
    z_gather_start(0)

    get_cinv.wait()
    span = nz * MODES
    for step in range(1, nx):
        src = m.mraw.at[:, pl.ds(pl.multiple_of(x_at(step) * span, BLOCK), span)]
        send(src, m.mt.at[xm], m.mss.at[step], m.mrs.at[step], x_peer(step))
    m.mt[xm] = m.mraw[:, pl.ds(pl.multiple_of(xm * span, BLOCK), span)]
    modes_at = [m.braw[:, rows(b)] for b in range(NBLOCKS)]
    for p in range(NBLOCKS):
        part = gathered(p, modes_at)
        high, low = split(part)
        m.bhl[0:MODES, rows(p)] = high
        m.bhl[MODES:2 * MODES, rows(p)] = low
        if p < 4:
            m.bfs[p] = part

    def in_blocks(source, into, combine):
        def step(i, carry):
            parts = [source[pl.ds(pl.multiple_of(b * BLOCK + i * 8, 8), 8), :] for b in range(NBLOCKS)]
            for p in range(NBLOCKS):
                into[pl.ds(pl.multiple_of(p * BLOCK + i * 8, 8), 8), :] = combine(p, parts)
            return carry
        lax.fori_loop(0, BLOCK // 8, step, 0)

    in_blocks(m.raw, m.r, gathered)
    for f in range(4):
        send(m.bfs.at[f], m.bfr.at[f ^ 1], m.bss.at[f], m.brs.at[f ^ 1], beside[f])
    for f in range(4):
        remote(m.r.at[rows(f), :], m.rp.at[rows(f ^ 1), :], m.rss.at[f], m.rrs.at[f ^ 1], beside[f]).start()

    def transposed(high, low):
        stacked = jnp.concatenate([high.astype(F32), low.astype(F32), high.astype(F32), jnp.zeros((MODES, BLOCK), F32)], axis=0)
        return stacked.T.astype(BF16)

    for p in range(NBLOCKS):
        m.bt[rows(p), :] = transposed(m.bhl[0:MODES, rows(p)], m.bhl[MODES:2 * MODES, rows(p)])
    m.yk[3 * MODES:, :] = jnp.zeros((MODES, width), BF16)

    get_comp.wait()
    def columns_in_order(i, carry):
        at = pl.ds(pl.multiple_of(i * 16, 16), 16)
        parts = [m.craw[at, rows(b)] for b in range(NBLOCKS)]
        values = [gathered(q, parts) for q in range(NBLOCKS)]
        for q in range(NBLOCKS):
            m.craw[at, rows(q)] = values[q]
        return carry

    def rows_in_order(i, carry):
        for q in range(NBLOCKS):
            parts = [m.craw[pl.ds(pl.multiple_of(b * BLOCK + i * 16, 16), 16), rows(q)] for b in range(NBLOCKS)]
            for p in range(NBLOCKS):
                at = pl.ds(pl.multiple_of(p * BLOCK + i * 16, 16), 16)
                high, low = split(gathered(p, parts))
                m.chi[at, rows(q)] = high
                m.clo[at, rows(q)] = low
        return carry

    lax.fori_loop(0, ORDER // 16, columns_in_order, 0)
    lax.fori_loop(0, BLOCK // 16, rows_in_order, 0)

    for step in range(1, nx):
        slot = m.mt.at[x_at(-step)]
        remote(slot, slot, m.mss.at[step], m.mrs.at[step], x_peer(step)).wait_recv()
    high, low = split(m.mt[...].reshape(nx * MODES, span))
    m.mhl[0:nx * MODES, :] = high
    m.mhl[nx * MODES:, :] = low
    for f in range(4):
        slot = m.bfr.at[f]
        remote(slot, slot, m.bss.at[f], m.brs.at[f], beside[f]).wait_recv()
        m.bpt[rows(f), :] = transposed(*split(m.bfr[f]))

    def stack_y(value):
        high, low = split(value)
        m.yk[0:MODES, :] = high
        m.yk[MODES:2 * MODES, :] = high
        m.yk[2 * MODES:3 * MODES, :] = low

    def solve_coarse(k):
        z_gather_wait(k)
        high, low = split(m.zg[k, :, 0:MODES, :].reshape(nz * MODES, width))
        both = mm(m.mhl[...], high)
        half = nx * MODES
        part = both[:half] + both[half:] + mm(m.mhl[0:half, :], low)
        m.xs[k, :, 0:MODES, :] = part.reshape(nx, MODES, width)
        sums = m.zg[k, 0, MODES:PACK, :]
        for j in range(1, nz):
            sums = sums + m.zg[k, j, MODES:PACK, :]
        for j in range(nx):
            m.xs[k, j, MODES:PACK, :] = sums
        for step in range(1, nx):
            send(m.xs.at[k, x_at(step)], m.xr.at[k, xm], m.xss.at[k, step], m.xrs.at[k, step], x_peer(step))
        m.xr[k, xm] = m.xs[k, xm]
        for step in range(1, nx):
            slot = m.xr.at[k, x_at(-step)]
            remote(slot, slot, m.xss.at[k, step], m.xrs.at[k, step], x_peer(step)).wait_recv()
        total = m.xr[k, 0]
        for j in range(1, nx):
            total = total + m.xr[k, j]
        m.yo[k] = total[:MODES]
        for f in range(4):
            send(m.yo.at[k], m.yp.at[k, f ^ 1], m.yss.at[k, f], m.yrs.at[k, f ^ 1], beside[f])
        stack_y(total[:MODES])
        return total[MODES:]

    def wait_y(k, f):
        slot = m.yp.at[k, f]
        remote(slot, slot, m.yss.at[k, f], m.yrs.at[k, f], beside[f]).wait_recv()

    def product(into, first, count, k_first, k_count, add):
        ks = pl.ds(k_first, k_count)
        size = 256
        def step(i, carry):
            at = pl.ds(pl.multiple_of(first + i * size, size), size)
            value = mm(m.chi[at, ks], m.vhi[ks, :]) + mm(m.chi[at, ks], m.vlo[ks, :]) + mm(m.clo[at, ks], m.vhi[ks, :])
            if add:
                value = value + into[at, :]
            into[at, :] = value
            return carry
        lax.fori_loop(0, count // size, step, 0)

    def coefficients(sums, old):
        rz, curve = sums[0:1], sums[1:2]
        if old is None:
            return rz, None, rz / curve
        ratio = rz / old[0]
        return rz, ratio, rz / (curve - ratio * rz / old[2])

    solve_coarse(0)
    coeff = None
    for k in range(ITERS):
        z = m.z.at[k]
        t = m.t.at[k]
        if k == 0:
            def new_z(at):
                z[at, :] = m.r[at, :] + mm(m.bt[at, :], m.yk[...])
        else:
            w = m.t.at[k - 1]
            z_old = m.z.at[k - 1]
            _, ratio, alpha = coeff

            def new_z(at, w=w, z_old=z_old, ratio=ratio, alpha=alpha, z=z):
                value = w[at, :] + mm(m.bt[at, :], m.yk[...])
                if ratio is not None:
                    value = value + ratio * m.q[at, :]
                m.q[at, :] = value
                z[at, :] = z_old[at, :] - alpha * value
        loop_rows(0, ORDER, new_z)
        loop_rows(FACE_ROWS, ORDER - FACE_ROWS, to_halves(z))
        product(t, 0, ORDER, FACE_ROWS, ORDER - FACE_ROWS, False)
        for f in range(4):
            wait_y(k, f)
            if k == 0:
                slot = m.rp.at[rows(f), :]
                copy = remote(slot, slot, m.rss.at[f], m.rrs.at[f], beside[f])
                copy.wait_recv()
                copy.wait_send()
            stack_y(m.yp[k, f])
            value = mm(m.bpt[rows(f), :], m.yk[...])
            if k == 0:
                value = m.rp[rows(f), :] + value
            else:
                value = m.wp[rows(f), :] + value
                if ratio is not None:
                    value = value + ratio * m.qp[rows(f), :]
                m.qp[rows(f), :] = value
                value = m.zp[rows(f), :] - alpha * value
            m.zp[rows(f), :] = value
            inner = z[rows(f), :] + halved(f, value)
            m.inner[rows(f), :] = inner
            high, low = split(inner)
            m.vhi[rows(f), :] = high
            m.vlo[rows(f), :] = low
        product(t, 0, FACE_ROWS, 0, FACE_ROWS, True)
        m.ts[k] = t[0:FACE_ROWS, :]
        for f in range(4):
            send(m.ts.at[k, rows(f), :], m.tp.at[k, rows(f ^ 1), :], m.tss.at[k, f], m.trs.at[k, f ^ 1], beside[f])
        product(t, FACE_ROWS, ORDER - FACE_ROWS, 0, FACE_ROWS, True)
        if k > 0:
            def update(at, w=w, z_old=z_old, ratio=ratio, alpha=alpha, first=(k == 1)):
                s_new, d_new = w[at, :], z_old[at, :]
                if ratio is not None:
                    s_new = s_new + ratio * m.s[at, :]
                    d_new = d_new + ratio * m.d[at, :]
                m.s[at, :] = s_new
                m.d[at, :] = d_new
                m.x[at, :] = alpha * d_new if first else m.x[at, :] + alpha * d_new
                m.r[at, :] = m.r[at, :] - alpha * s_new
            loop_rows(0, ORDER, update)

        def dots(i, carry, z=z, t=t):
            at = pl.ds(pl.multiple_of(i * CHUNK, CHUNK), CHUNK)
            low_at = pl.ds(pl.multiple_of(FACE_ROWS + i * CHUNK, CHUNK), CHUNK)
            first = carry[0] + fold(m.r[at, :] * z[at, :]) + fold(m.r[low_at, :] * z[low_at, :])
            second = carry[1] + fold(m.inner[at, :] * t[at, :]) + fold(z[low_at, :] * t[low_at, :])
            return first, second
        zero = jnp.zeros((8, width), F32)
        first, second = lax.fori_loop(0, FACE_ROWS // CHUNK, dots, (zero, zero))
        m.cd[k, c, 0:1, :] = jnp.sum(first, axis=0, keepdims=True)
        m.cd[k, c, 1:2, :] = jnp.sum(second, axis=0, keepdims=True)
        m.cd[k, c, 2:8, :] = jnp.zeros((6, width), F32)
        for step in range(1, nc):
            mine = m.cd.at[k, c]
            send(mine, mine, m.css.at[k, step], m.crs.at[k, step], c_peer(step))
        if k + 1 < ITERS:
            loop_rows(FACE_ROWS, ORDER - FACE_ROWS, to_halves(t))
            inside = coarse(FACE_ROWS, ORDER - FACE_ROWS)
        for f in range(4):
            slot = m.tp.at[k, rows(f), :]
            remote(slot, slot, m.tss.at[k, f], m.trs.at[k, f], beside[f]).wait_recv()
            own = m.ts[k, rows(f), :]
            theirs = m.tp[k, rows(f), :]
            value = own + halved(f, theirs)
            t[rows(f), :] = value
            if k + 1 < ITERS:
                m.wp[rows(f), :] = theirs + halved(f, own)
                high, low = split(value)
                m.vhi[rows(f), :] = high
                m.vlo[rows(f), :] = low
        for step in range(1, nc):
            slot = m.cd.at[k, c_at(-step)]
            remote(slot, slot, m.css.at[k, step], m.crs.at[k, step], c_peer(step)).wait_recv()
        sums = m.cd[k, 0]
        for j in range(1, nc):
            sums = sums + m.cd[k, j]
        if k + 1 < ITERS:
            m.zg[k + 1, zm, 0:MODES, :] = inside + coarse(0, FACE_ROWS)
            m.zg[k + 1, zm, MODES:PACK, :] = sums
            z_gather_start(k + 1)
            coeff = coefficients(solve_coarse(k + 1), coeff)

    m.zd[zm] = sums
    for step in far_first:
        mine = m.zd.at[zm]
        send(mine, mine, m.fzs.at[step], m.fzr.at[step], z_peer(step))
    z = m.z.at[ITERS - 1]
    t = m.t.at[ITERS - 1]
    for j, source in enumerate((m.x, z, m.d, m.r, t, m.s)):
        in_blocks(source, m.out.at[j], scattered)
    for step in reversed(far_first):
        slot = m.zd.at[z_at(-step)]
        remote(slot, slot, m.fzs.at[step], m.fzr.at[step], z_peer(step)).wait_recv()
    sums = m.zd[0]
    for j in range(1, nz):
        sums = sums + m.zd[j]
    m.xd[xm] = sums
    for step in range(1, nx):
        mine = m.xd.at[xm]
        send(mine, mine, m.fxs.at[step], m.fxr.at[step], x_peer(step))
    for step in range(1, nx):
        slot = m.xd.at[x_at(-step)]
        remote(slot, slot, m.fxs.at[step], m.fxr.at[step], x_peer(step)).wait_recv()
    sums = m.xd[0]
    for j in range(1, nx):
        sums = sums + m.xd[j]
    _, ratio, alpha = coefficients(sums, coeff)
    def finish(at):
        x_out[0, 0, at, :] = m.out[0, at, :] + alpha * (m.out[1, at, :] + ratio * m.out[2, at, :])
        r_out[0, 0, at, :] = m.out[3, at, :] - alpha * (m.out[4, at, :] + ratio * m.out[5, at, :])
    loop_rows(0, ORDER, finish)
    for copy in pending:
        copy.wait_send()


class Names:
    def __init__(self, names, refs):
        for name, ref in zip(names, refs, strict=True):
            setattr(self, name, ref)


def scratch(nx, nz, nc, width):
    vmem, dma = pltpu.VMEM, pltpu.SemaphoreType.DMA
    span = nz * MODES
    full, face = (ORDER, width), (FACE_ROWS, width)
    return dict(
        raw=vmem(full, F32), braw=vmem((MODES, ORDER), F32), mraw=vmem((MODES, nx * span), F32), craw=vmem((ORDER, ORDER), F32),
        fbs=pltpu.SMEM((nx * nz, 4), jnp.int32), ers=pltpu.SMEM((2, nx * nz, 2), jnp.int32),
        chi=vmem((ORDER, ORDER), BF16), clo=vmem((ORDER, ORDER), BF16), vhi=vmem(full, BF16), vlo=vmem(full, BF16),
        bhl=vmem((2 * MODES, ORDER), BF16), bt=vmem((ORDER, BLOCK), BF16), bpt=vmem((FACE_ROWS, BLOCK), BF16),
        yk=vmem((BLOCK, width), BF16), mt=vmem((nx, MODES, span), F32), mhl=vmem((2 * nx * MODES, span), BF16),
        zg=vmem((ITERS, nz, PACK, width), F32), xs=vmem((ITERS, nx, PACK, width), F32), xr=vmem((ITERS, nx, PACK, width), F32),
        yo=vmem((ITERS, MODES, width), F32), yp=vmem((ITERS, 4, MODES, width), F32),
        ts=vmem((ITERS, *face), F32), tp=vmem((ITERS, *face), F32), cd=vmem((ITERS, nc, SUMS, width), F32),
        zd=vmem((nz, SUMS, width), F32), xd=vmem((nx, SUMS, width), F32),
        bfs=vmem((4, MODES, BLOCK), F32), bfr=vmem((4, MODES, BLOCK), F32), rp=vmem(face, F32),
        z=vmem((ITERS, *full), F32), t=vmem((ITERS, *full), F32), q=vmem(full, F32), s=vmem(full, F32), r=vmem(full, F32),
        d=vmem(full, F32), x=vmem(full, F32), zp=vmem(face, F32), qp=vmem(face, F32), wp=vmem(face, F32), inner=vmem(face, F32), weight=vmem(face, F32), out=vmem((6, *full), F32),
        lsem=dma((8,)), zss=dma((ITERS, nz)), zrs=dma((ITERS, nz)), xss=dma((ITERS, nx)), xrs=dma((ITERS, nx)),
        yss=dma((ITERS, 4)), yrs=dma((ITERS, 4)), tss=dma((ITERS, 4)), trs=dma((ITERS, 4)), css=dma((ITERS, nc)), crs=dma((ITERS, nc)),
        fzs=dma((nz,)), fzr=dma((nz,)), fxs=dma((nx,)), fxr=dma((nx,)), mss=dma((nx,)), mrs=dma((nx,)),
        bss=dma((4,)), brs=dma((4,)), rss=dma((4,)), rrs=dma((4,)),
    )


def shards(nx, nz, nc, compliance, loads, modes, coarse_inverse, face_block, edge_rows):
    width = loads.shape[-1]
    held = scratch(nx, nz, nc, width)

    def body(*refs):
        kernel(nx, nz, nc, *refs[:8], Names(held, refs[8:]))

    anywhere = pl.BlockSpec(memory_space=pl.ANY)
    return pl.pallas_call(
        body,
        out_shape=[jax.ShapeDtypeStruct(loads.shape, F32)] * 2,
        in_specs=[anywhere] * 6,
        out_specs=[pl.BlockSpec(memory_space=pltpu.VMEM)] * 2,
        scratch_shapes=list(held.values()),
        compiler_params=pltpu.CompilerParams(collective_id=0, has_side_effects=True, vmem_limit_bytes=56 * 1024 * 1024),
    )(compliance, loads, modes, coarse_inverse, face_block, edge_rows)


def solution(mesh, nz=NZ):
    nc, ns = mesh.shape["cluster"], mesh.shape["sub"]
    cut = P("cluster", "sub", None, None)
    return jax.shard_map(
        functools.partial(shards, ns // nz, nz, nc), mesh=mesh,
        in_specs=(cut, cut, cut, P("cluster", "sub", None), P(), P()),
        out_specs=(cut, cut), check_vma=False,
    )
```

```python
import functools

import jax
import jax.numpy as jnp
from jax import lax
from jax.experimental import pallas as pl
from jax.experimental.pallas import tpu as pltpu
from jax.sharding import PartitionSpec as P

BLOCK = 128
NBLOCKS = 8
ORDER = BLOCK * NBLOCKS
FACE_ROWS = 4 * BLOCK
MODES = 32
SUMS = 8
PACK = MODES + SUMS
ITERS = 3
NZ = 8
CHUNK = 64
WIDE = 256
F32 = jnp.float32
BF16 = jnp.bfloat16


def split(value):
    high = value.astype(BF16)
    return high, (value - high.astype(F32)).astype(BF16)


def mm(left, right):
    return jnp.dot(left, right, preferred_element_type=F32)


def same(left, right):
    gap = left - right
    return 1 - jnp.minimum(gap * gap, 1)


def fold(value):
    rows, width = value.shape
    return jnp.sum(value.reshape(rows // 8, 8, width), axis=0)


def remote(src, dst, send_sem, recv_sem, device):
    return pltpu.make_async_remote_copy(
        src_ref=src, dst_ref=dst, send_sem=send_sem, recv_sem=recv_sem,
        device_id=device, device_id_type=pl.DeviceIdType.MESH,
    )


def kernel(nx, nz, nc, comp, loads, modes, cinv, fb, er, x_out, r_out, place_out, m):
    ns = nx * nz
    c = lax.axis_index("cluster")
    s = lax.axis_index("sub")
    xm = lax.div(s, nz)
    zm = lax.rem(s, nz)
    width = m.raw.shape[1]

    def z_at(step):
        return lax.rem(zm + (step + nz), nz)

    def x_at(step):
        return lax.rem(xm + (step + nx), nx)

    def c_at(step):
        return lax.rem(c + (step + nc), nc)

    def z_peer(step):
        return (c, xm * nz + z_at(step))

    def x_peer(step):
        return (c, x_at(step) * nz + zm)

    def c_peer(step):
        return (c_at(step), s)

    beside = (
        (c, lax.rem(s + ns - 1, ns)),
        (c, lax.rem(s + 1, ns)),
        (c_at(-1), s),
        (c_at(1), s),
    )

    get_loads = pltpu.make_async_copy(loads.at[0, 0], m.raw, m.lsem.at[0])
    get_modes = pltpu.make_async_copy(modes.at[0, 0], m.braw, m.lsem.at[1])
    get_cinv = pltpu.make_async_copy(cinv.at[0], m.mraw, m.lsem.at[2])
    get_comp = pltpu.make_async_copy(comp.at[0, 0], m.craw, m.lsem.at[3])
    get_fb = pltpu.make_async_copy(fb.at[c], m.fbs, m.lsem.at[4])
    get_er = pltpu.make_async_copy(er.at[c], m.ers.at[0], m.lsem.at[5])
    get_er_low = pltpu.make_async_copy(er.at[jnp.maximum(c - 1, 0)], m.ers.at[1], m.lsem.at[6])
    for copy in (get_fb, get_er, get_er_low, get_loads, get_modes, get_cinv, get_comp):
        copy.start()

    barrier = pltpu.get_barrier_semaphore()
    greeted = (
        [z_peer(step) for step in range(1, nz)]
        + [x_peer(step) for step in range(1, nx)]
        + [c_peer(step) for step in range(1, nc)]
        + [beside[0], beside[1]]
    )
    for peer in greeted:
        pl.semaphore_signal(barrier, inc=1, device_id=peer, device_id_type=pl.DeviceIdType.MESH)

    for copy in (get_fb, get_er, get_er_low):
        copy.wait()
    faces = [m.fbs[f, s] for f in range(4)]
    rank = jnp.int32(0)
    place = [jnp.int32(0)] * NBLOCKS
    pick = [[] for _ in range(NBLOCKS)]
    for b in range(NBLOCKS):
        hits = [same(face, b) for face in faces]
        free = 1 - (hits[0] + hits[1] + hits[2] + hits[3])
        hits = hits + [free * same(rank, j) for j in range(4)]
        for p in range(NBLOCKS):
            pick[p].append(hits[p].astype(F32))
            place[p] = place[p] + b * hits[p]
        rank = rank + free

    def gathered(p, parts):
        value = pick[p][0] * parts[0]
        for b in range(1, NBLOCKS):
            value = value + pick[p][b] * parts[b]
        return value

    for p in range(NBLOCKS):
        place_out[p] = place[p]

    shared = [
        m.ers[0, 0, jnp.maximum(s - 1, 0)] * jnp.minimum(s, 1),
        m.ers[0, 0, s] * jnp.minimum(ns - 1 - s, 1),
        m.ers[1, 1, s] * jnp.minimum(c, 1),
        m.ers[0, 1, s] * jnp.minimum(nc - 1 - c, 1),
    ]
    row_at = lax.broadcasted_iota(jnp.int32, (BLOCK, width), 0)
    for f in range(4):
        m.weight[pl.ds(f * BLOCK, BLOCK), :] = 0.5 * jnp.clip(shared[f] - row_at, 0, 1).astype(F32)

    def halved(face, value):
        return m.weight[pl.ds(face * BLOCK, BLOCK), :] * value

    def rows(p):
        return pl.ds(p * BLOCK, BLOCK)

    def loop_rows(first, count, body):
        def step(i, carry):
            body(pl.ds(pl.multiple_of(first + i * CHUNK, CHUNK), CHUNK))
            return carry
        lax.fori_loop(0, count // CHUNK, step, 0)

    def to_halves(source):
        def body(at):
            high, low = split(source[at, :])
            m.vhi[at, :] = high
            m.vlo[at, :] = low
        return body

    get_modes.wait()
    high, low = split(m.braw[...])
    m.bhl[0:MODES, :] = high
    m.bhl[MODES:2 * MODES, :] = low
    get_loads.wait()
    loop_rows(0, ORDER, to_halves(m.raw))

    def coarse(first, count):
        ks = pl.ds(first, count)
        both = mm(m.bhl[:, ks], m.vhi[ks, :])
        return both[:MODES] + both[MODES:] + mm(m.bhl[0:MODES, ks], m.vlo[ks, :])

    pending = []

    def send(src, dst, send_sem, recv_sem, device):
        copy = remote(src, dst, send_sem, recv_sem, device)
        copy.start()
        pending.append(copy)

    far_first = sorted(range(1, nz), key=lambda step: -min(step, nz - step))

    early = 24

    def z_gather_start(k):
        for step in (2, nz - 2, 1, nz - 1):
            mine = m.zg.at[k, zm]
            send(mine, mine, m.zss.at[k, step], m.zrs.at[k, step], z_peer(step))

    def z_wait(k, step, sem, first=0, count=PACK):
        slot = m.zg.at[k, z_at(-step), pl.ds(first, count), :]
        remote(slot, slot, m.zss.at[k, sem], m.zrs.at[k, sem], z_peer(step)).wait_recv()

    def z_gather_forward(k):
        for sign, first, count, sem in ((1, 0, early, 4), (-1, early, PACK - early, nz)):
            z_wait(k, 2 * sign, (2 * sign) % nz)
            slot = m.zg.at[k, z_at(-2 * sign)]
            step = (3 * sign) % nz
            send(slot, slot, m.zss.at[k, step], m.zrs.at[k, step], z_peer(sign))
            slot = m.zg.at[k, z_at(-2 * sign), pl.ds(first, count), :]
            send(slot, slot, m.zss.at[k, sem], m.zrs.at[k, sem], z_peer(2 * sign))

    def z_gather_wait(k):
        for step in (1, -1, 3, -3):
            z_wait(k, step, step % nz)
        z_wait(k, 4, 4, 0, early)
        z_wait(k, 4, nz, early, PACK - early)

    m.zg[0, zm, 0:MODES, :] = coarse(0, ORDER)
    m.zg[0, zm, MODES:PACK, :] = jnp.zeros((SUMS, width), F32)
    pl.semaphore_wait(barrier, len(greeted))
    z_gather_start(0)

    get_cinv.wait()
    span = nz * MODES
    for step in range(1, nx):
        src = m.mraw.at[:, pl.ds(pl.multiple_of(x_at(step) * span, BLOCK), span)]
        send(src, m.mt.at[xm], m.mss.at[step], m.mrs.at[step], x_peer(step))
    m.mt[xm] = m.mraw[:, pl.ds(pl.multiple_of(xm * span, BLOCK), span)]
    modes_at = [m.braw[:, rows(b)] for b in range(NBLOCKS)]
    for p in range(NBLOCKS):
        part = gathered(p, modes_at)
        high, low = split(part)
        m.bhl[0:MODES, rows(p)] = high
        m.bhl[MODES:2 * MODES, rows(p)] = low
        if p < 4:
            m.bfs[p] = part

    def in_blocks(source, into, combine):
        def step(i, carry):
            parts = [source[pl.ds(pl.multiple_of(b * BLOCK + i * 8, 8), 8), :] for b in range(NBLOCKS)]
            for p in range(NBLOCKS):
                into[pl.ds(pl.multiple_of(p * BLOCK + i * 8, 8), 8), :] = combine(p, parts)
            return carry
        lax.fori_loop(0, BLOCK // 8, step, 0)

    in_blocks(m.raw, m.r, gathered)
    z_gather_forward(0)
    for f in range(4):
        send(m.bfs.at[f], m.bfr.at[f ^ 1], m.bss.at[f], m.brs.at[f ^ 1], beside[f])
    for f in range(4):
        remote(m.r.at[rows(f), :], m.rp.at[rows(f ^ 1), :], m.rss.at[f], m.rrs.at[f ^ 1], beside[f]).start()

    def transposed(high, low):
        stacked = jnp.concatenate([high.astype(F32), low.astype(F32), high.astype(F32), jnp.zeros((MODES, BLOCK), F32)], axis=0)
        return stacked.T.astype(BF16)

    for p in range(NBLOCKS):
        m.bt[rows(p), :] = transposed(m.bhl[0:MODES, rows(p)], m.bhl[MODES:2 * MODES, rows(p)])
    m.yk[:, 3 * MODES:, :] = jnp.zeros((5, MODES, width), BF16)

    get_comp.wait()
    def columns_in_order(i, carry):
        at = pl.ds(pl.multiple_of(i * 16, 16), 16)
        parts = [m.craw[at, rows(b)] for b in range(NBLOCKS)]
        values = [gathered(q, parts) for q in range(NBLOCKS)]
        for q in range(NBLOCKS):
            m.craw[at, rows(q)] = values[q]
        return carry

    def rows_in_order(i, carry):
        for q in range(NBLOCKS):
            parts = [m.craw[pl.ds(pl.multiple_of(b * BLOCK + i * 16, 16), 16), rows(q)] for b in range(NBLOCKS)]
            for p in range(NBLOCKS):
                at = pl.ds(pl.multiple_of(p * BLOCK + i * 16, 16), 16)
                high, low = split(gathered(p, parts))
                m.chi[at, rows(q)] = high
                m.clo[at, rows(q)] = low
        return carry

    lax.fori_loop(0, ORDER // 16, columns_in_order, 0)
    lax.fori_loop(0, BLOCK // 16, rows_in_order, 0)

    for step in range(1, nx):
        slot = m.mt.at[x_at(-step)]
        remote(slot, slot, m.mss.at[step], m.mrs.at[step], x_peer(step)).wait_recv()
    high, low = split(m.mt[...].reshape(nx * MODES, span))
    m.mhl[0:nx * MODES, :] = high
    m.mhl[nx * MODES:, :] = low
    for f in range(4):
        slot = m.bfr.at[f]
        remote(slot, slot, m.bss.at[f], m.brs.at[f], beside[f]).wait_recv()
        m.bpt[rows(f), :] = transposed(*split(m.bfr[f]))

    def stack_y(i, value):
        high, low = split(value)
        m.yk[i, 0:MODES, :] = high
        m.yk[i, MODES:2 * MODES, :] = high
        m.yk[i, 2 * MODES:3 * MODES, :] = low

    def solve_coarse(k):
        z_gather_wait(k)
        high, low = split(m.zg[k, :, 0:MODES, :].reshape(nz * MODES, width))
        both = mm(m.mhl[...], high)
        half = nx * MODES
        part = both[:half] + both[half:] + mm(m.mhl[0:half, :], low)
        m.xs[k, :, 0:MODES, :] = part.reshape(nx, MODES, width)
        sums = m.zg[k, 0, MODES:PACK, :]
        for j in range(1, nz):
            sums = sums + m.zg[k, j, MODES:PACK, :]
        for j in range(nx):
            m.xs[k, j, MODES:PACK, :] = sums
        for step in range(1, nx):
            send(m.xs.at[k, x_at(step)], m.xr.at[k, xm], m.xss.at[k, step], m.xrs.at[k, step], x_peer(step))
        m.xr[k, xm] = m.xs[k, xm]
        for step in range(1, nx):
            slot = m.xr.at[k, x_at(-step)]
            remote(slot, slot, m.xss.at[k, step], m.xrs.at[k, step], x_peer(step)).wait_recv()
        total = m.xr[k, 0]
        for j in range(1, nx):
            total = total + m.xr[k, j]
        m.yo[k] = total[:MODES]
        for f in range(4):
            send(m.yo.at[k], m.yp.at[k, f ^ 1], m.yss.at[k, f], m.yrs.at[k, f ^ 1], beside[f])
        stack_y(4, total[:MODES])
        return total[MODES:]

    def wait_y(k, f):
        slot = m.yp.at[k, f]
        remote(slot, slot, m.yss.at[k, f], m.yrs.at[k, f], beside[f]).wait_recv()

    def product(at, ks):
        return mm(m.chi[at, ks], m.vhi[ks, :]) + mm(m.chi[at, ks], m.vlo[ks, :]) + mm(m.clo[at, ks], m.vhi[ks, :])

    def keep_halves(at, value):
        high, low = split(value)
        m.vhi[at, :] = high
        m.vlo[at, :] = low

    near, inside = pl.ds(0, FACE_ROWS), pl.ds(FACE_ROWS, ORDER - FACE_ROWS)
    near_parts = [pl.ds(i, WIDE) for i in range(0, FACE_ROWS, WIDE)]
    inside_parts = [pl.ds(i, WIDE) for i in range(FACE_ROWS, ORDER, WIDE)]

    def coefficients(sums, old):
        rz, curve = sums[0:1], sums[1:2]
        if old is None:
            return rz, None, rz / curve
        ratio = rz / old[0]
        return rz, ratio, rz / (curve - ratio * rz / old[2])

    solve_coarse(0)
    coeff = None
    for k in range(ITERS):
        z = m.z.at[k]
        t = m.t.at[k]
        if k > 0:
            w = m.t.at[k - 1]
            z_old = m.z.at[k - 1]
            _, ratio, alpha = coeff
        for at in inside_parts + near_parts:
            value = mm(m.bt[at, :], m.yk[4])
            if k == 0:
                value = m.r[at, :] + value
            else:
                value = w[at, :] + value
                if ratio is not None:
                    value = value + ratio * m.q[at, :]
                m.q[at, :] = value
                value = z_old[at, :] - alpha * value
            z[at, :] = value
            if at in inside_parts:
                keep_halves(at, value)
        for at in near_parts + inside_parts:
            t[at, :] = product(at, inside)
        def update(i, total, z=z):
            at = pl.ds(pl.multiple_of(i * CHUNK, CHUNK), CHUNK)
            r = m.r[at, :]
            if k > 0:
                s_new, d_new = w[at, :], z_old[at, :]
                if ratio is not None:
                    s_new = s_new + ratio * m.s[at, :]
                    d_new = d_new + ratio * m.d[at, :]
                m.s[at, :] = s_new
                m.d[at, :] = d_new
                m.x[at, :] = alpha * d_new if k == 1 else m.x[at, :] + alpha * d_new
                r = r - alpha * s_new
                m.r[at, :] = r
            return total + fold(r * z[at, :])
        zero = jnp.zeros((8, width), F32)
        first = lax.fori_loop(0, ORDER // CHUNK, update, zero)
        m.cd[k, c, 0:1, :] = jnp.sum(first, axis=0, keepdims=True)
        m.cd[k, c, 2:8, :] = jnp.zeros((6, width), F32)
        for f in (2, 3, 0, 1):
            wait_y(k, f)
            if k == 0:
                slot = m.rp.at[rows(f), :]
                copy = remote(slot, slot, m.rss.at[f], m.rrs.at[f], beside[f])
                copy.wait_recv()
                copy.wait_send()
        for f in range(4):
            stack_y(f, m.yp[k, f])
        for f in range(4):
            value = mm(m.bpt[rows(f), :], m.yk[f])
            if k == 0:
                value = m.rp[rows(f), :] + value
            else:
                value = m.wp[rows(f), :] + value
                if ratio is not None:
                    value = value + ratio * m.qp[rows(f), :]
                m.qp[rows(f), :] = value
                value = m.zp[rows(f), :] - alpha * value
            m.zp[rows(f), :] = value
            inner = z[rows(f), :] + halved(f, value)
            m.inner[rows(f), :] = inner
            keep_halves(rows(f), inner)
        for at in near_parts:
            m.ts[k, at, :] = t[at, :] + product(at, near)
        for f in range(4):
            send(m.ts.at[k, rows(f), :], m.tp.at[k, rows(f ^ 1), :], m.tss.at[k, f], m.trs.at[k, f ^ 1], beside[f])
        for at in inside_parts:
            value = t[at, :] + product(at, near)
            t[at, :] = value
            if k + 1 < ITERS:
                keep_halves(at, value)

        def dots(i, total, z=z, t=t, k=k):
            at = pl.ds(pl.multiple_of(i * CHUNK, CHUNK), CHUNK)
            low_at = pl.ds(pl.multiple_of(FACE_ROWS + i * CHUNK, CHUNK), CHUNK)
            return total + fold(m.inner[at, :] * m.ts[k, at, :]) + fold(z[low_at, :] * t[low_at, :])
        second = lax.fori_loop(0, FACE_ROWS // CHUNK, dots, zero)
        m.cd[k, c, 1:2, :] = jnp.sum(second, axis=0, keepdims=True)
        for step in range(1, nc):
            mine = m.cd.at[k, c]
            send(mine, mine, m.css.at[k, step], m.crs.at[k, step], c_peer(step))
        if k + 1 < ITERS:
            part = coarse(FACE_ROWS, ORDER - FACE_ROWS)
        for f in range(4):
            slot = m.tp.at[k, rows(f), :]
            remote(slot, slot, m.tss.at[k, f], m.trs.at[k, f], beside[f]).wait_recv()
        for f in range(4):
            own = m.ts[k, rows(f), :]
            theirs = m.tp[k, rows(f), :]
            value = own + halved(f, theirs)
            t[rows(f), :] = value
            if k + 1 < ITERS:
                m.wp[rows(f), :] = theirs + halved(f, own)
                keep_halves(rows(f), value)
        if k + 1 < ITERS:
            part = part + coarse(0, FACE_ROWS)
        for step in range(1, nc):
            slot = m.cd.at[k, c_at(-step)]
            remote(slot, slot, m.css.at[k, step], m.crs.at[k, step], c_peer(step)).wait_recv()
        sums = m.cd[k, 0]
        for j in range(1, nc):
            sums = sums + m.cd[k, j]
        if k + 1 < ITERS:
            m.zg[k + 1, zm, 0:MODES, :] = part
            m.zg[k + 1, zm, MODES:PACK, :] = sums
            z_gather_start(k + 1)
            z_gather_forward(k + 1)
            coeff = coefficients(solve_coarse(k + 1), coeff)

    m.zd[zm] = sums
    for step in far_first:
        mine = m.zd.at[zm]
        send(mine, mine, m.fzs.at[step], m.fzr.at[step], z_peer(step))
    for step in reversed(far_first):
        slot = m.zd.at[z_at(-step)]
        remote(slot, slot, m.fzs.at[step], m.fzr.at[step], z_peer(step)).wait_recv()
    sums = m.zd[0]
    for j in range(1, nz):
        sums = sums + m.zd[j]
    m.xd[xm] = sums
    for step in range(1, nx):
        mine = m.xd.at[xm]
        send(mine, mine, m.fxs.at[step], m.fxr.at[step], x_peer(step))
    for step in range(1, nx):
        slot = m.xd.at[x_at(-step)]
        remote(slot, slot, m.fxs.at[step], m.fxr.at[step], x_peer(step)).wait_recv()
    sums = m.xd[0]
    for j in range(1, nx):
        sums = sums + m.xd[j]
    _, ratio, alpha = coefficients(sums, coeff)
    z = m.z.at[ITERS - 1]
    t = m.t.at[ITERS - 1]

    def finish(at):
        m.out[0, at, :] = m.x[at, :] + alpha * (z[at, :] + ratio * m.d[at, :])
        m.out[1, at, :] = m.r[at, :] - alpha * (t[at, :] + ratio * m.s[at, :])
    half = ORDER // 2
    outs = []
    for i in range(2):
        loop_rows(i * half, half, finish)
        at = pl.ds(i * half, half)
        for j, into in enumerate((x_out, r_out)):
            outs.append(pltpu.make_async_copy(m.out.at[j, at, :], into.at[0, 0, at, :], m.lsem.at[2 * i + j]))
            outs[-1].start()
    for copy in outs:
        copy.wait()
    for copy in pending:
        copy.wait_send()


class Names:
    def __init__(self, names, refs):
        for name, ref in zip(names, refs, strict=True):
            setattr(self, name, ref)


def scratch(nx, nz, nc, width):
    vmem, dma = pltpu.VMEM, pltpu.SemaphoreType.DMA
    span = nz * MODES
    full, face = (ORDER, width), (FACE_ROWS, width)
    return dict(
        raw=vmem(full, F32), braw=vmem((MODES, ORDER), F32), mraw=vmem((MODES, nx * span), F32), craw=vmem((ORDER, ORDER), F32),
        fbs=pltpu.SMEM((4, nx * nz), jnp.int32), ers=pltpu.SMEM((2, 2, nx * nz), jnp.int32),
        chi=vmem((ORDER, ORDER), BF16), clo=vmem((ORDER, ORDER), BF16), vhi=vmem(full, BF16), vlo=vmem(full, BF16),
        bhl=vmem((2 * MODES, ORDER), BF16), bt=vmem((ORDER, BLOCK), BF16), bpt=vmem((FACE_ROWS, BLOCK), BF16),
        yk=vmem((5, BLOCK, width), BF16), mt=vmem((nx, MODES, span), F32), mhl=vmem((2 * nx * MODES, span), BF16),
        zg=vmem((ITERS, nz, PACK, width), F32), xs=vmem((ITERS, nx, PACK, width), F32), xr=vmem((ITERS, nx, PACK, width), F32),
        yo=vmem((ITERS, MODES, width), F32), yp=vmem((ITERS, 4, MODES, width), F32),
        ts=vmem((ITERS, *face), F32), tp=vmem((ITERS, *face), F32), cd=vmem((ITERS, nc, SUMS, width), F32),
        zd=vmem((nz, SUMS, width), F32), xd=vmem((nx, SUMS, width), F32),
        bfs=vmem((4, MODES, BLOCK), F32), bfr=vmem((4, MODES, BLOCK), F32), rp=vmem(face, F32),
        z=vmem((ITERS, *full), F32), t=vmem((ITERS, *full), F32), q=vmem(full, F32), s=vmem(full, F32), r=vmem(full, F32),
        d=vmem(full, F32), x=vmem(full, F32), zp=vmem(face, F32), qp=vmem(face, F32), wp=vmem(face, F32), inner=vmem(face, F32), weight=vmem(face, F32), out=vmem((2, *full), F32),
        lsem=dma((8,)), zss=dma((ITERS, nz + 1)), zrs=dma((ITERS, nz + 1)), xss=dma((ITERS, nx)), xrs=dma((ITERS, nx)),
        yss=dma((ITERS, 4)), yrs=dma((ITERS, 4)), tss=dma((ITERS, 4)), trs=dma((ITERS, 4)), css=dma((ITERS, nc)), crs=dma((ITERS, nc)),
        fzs=dma((nz,)), fzr=dma((nz,)), fxs=dma((nx,)), fxr=dma((nx,)), mss=dma((nx,)), mrs=dma((nx,)),
        bss=dma((4,)), brs=dma((4,)), rss=dma((4,)), rrs=dma((4,)),
    )


def back_in_place(place, x, r, x_out, r_out, sems):
    copies = []
    for p in range(NBLOCKS):
        at = pl.ds(pl.multiple_of(place[p] * BLOCK, BLOCK), BLOCK)
        for j, (source, into) in enumerate(((x, x_out), (r, r_out))):
            copies.append(pltpu.make_async_copy(source.at[0, 0, pl.ds(p * BLOCK, BLOCK), :], into.at[0, 0, at, :], sems.at[j, p]))
            copies[-1].start()
    for copy in copies:
        copy.wait()


def shards(nx, nz, nc, compliance, loads, modes, coarse_inverse, face_block, edge_rows):
    width = loads.shape[-1]
    held = scratch(nx, nz, nc, width)

    def body(*refs):
        kernel(nx, nz, nc, *refs[:9], Names(held, refs[9:]))

    anywhere = pl.BlockSpec(memory_space=pl.ANY)
    small = pl.BlockSpec(memory_space=pltpu.SMEM)
    shapes = [jax.ShapeDtypeStruct(loads.shape, F32)] * 2
    x, r, place = pl.pallas_call(
        body,
        out_shape=shapes + [jax.ShapeDtypeStruct((NBLOCKS,), jnp.int32)],
        in_specs=[anywhere] * 6,
        out_specs=[anywhere, anywhere, small],
        scratch_shapes=list(held.values()),
        compiler_params=pltpu.CompilerParams(collective_id=0, has_side_effects=True, vmem_limit_bytes=56 * 1024 * 1024),
    )(compliance, loads, modes, coarse_inverse, jnp.transpose(face_block, (0, 2, 1)), jnp.transpose(edge_rows, (0, 2, 1)))
    return pl.pallas_call(
        back_in_place,
        out_shape=shapes,
        in_specs=[small, anywhere, anywhere],
        out_specs=[anywhere, anywhere],
        scratch_shapes=[pltpu.SemaphoreType.DMA((2, NBLOCKS))],
    )(place, x, r)


def solution(mesh, nz=NZ):
    nc, ns = mesh.shape["cluster"], mesh.shape["sub"]
    cut = P("cluster", "sub", None, None)
    return jax.shard_map(
        functools.partial(shards, ns // nz, nz, nc), mesh=mesh,
        in_specs=(cut, cut, cut, P("cluster", "sub", None), P(), P()),
        out_specs=(cut, cut), check_vma=False,
    )
```

```python
import functools

import jax
import jax.numpy as jnp
from jax import lax
from jax.experimental import pallas as pl
from jax.experimental.pallas import tpu as pltpu
from jax.sharding import PartitionSpec as P

BLOCK = 128
NBLOCKS = 8
ORDER = BLOCK * NBLOCKS
FACE_ROWS = 4 * BLOCK
MODES = 32
SUMS = 2
PACK = MODES + 8
ITERS = 3
NZ = 8
CHUNK = 64
WIDE = 256
F32 = jnp.float32
BF16 = jnp.bfloat16


def split(value):
    high = value.astype(BF16)
    return high, (value - high.astype(F32)).astype(BF16)


def mm(left, right):
    return jnp.dot(left, right, preferred_element_type=F32)


def same(left, right):
    gap = left - right
    return 1 - jnp.minimum(gap * gap, 1)


def fold(value):
    rows, width = value.shape
    return jnp.sum(value.reshape(rows // 8, 8, width), axis=0)


def remote(src, dst, send_sem, recv_sem, device):
    return pltpu.make_async_remote_copy(
        src_ref=src, dst_ref=dst, send_sem=send_sem, recv_sem=recv_sem,
        device_id=device, device_id_type=pl.DeviceIdType.MESH,
    )


def kernel(nx, nz, nc, comp, loads, modes, cinv, fb, er, x_out, r_out, place_out, m):
    ns = nx * nz
    c = lax.axis_index("cluster")
    s = lax.axis_index("sub")
    xm = lax.div(s, nz)
    zm = lax.rem(s, nz)
    width = m.raw.shape[1]

    def z_at(step):
        return lax.rem(zm + (step + nz), nz)

    def x_at(step):
        return lax.rem(xm + (step + nx), nx)

    def c_at(step):
        return lax.rem(c + (step + nc), nc)

    def z_peer(step):
        return (c, xm * nz + z_at(step))

    def x_peer(step):
        return (c, x_at(step) * nz + zm)

    def c_peer(step):
        return (c_at(step), s)

    def cx_peer(step):
        return (c_at(step[0]), x_at(step[1]) * nz + zm)

    beside = (
        (c, lax.rem(s + ns - 1, ns)),
        (c, lax.rem(s + 1, ns)),
        (c_at(-1), s),
        (c_at(1), s),
    )

    get_loads = pltpu.make_async_copy(loads.at[0, 0], m.raw, m.lsem.at[0])
    get_modes = pltpu.make_async_copy(modes.at[0, 0], m.braw, m.lsem.at[1])
    get_cinv = pltpu.make_async_copy(cinv.at[0], m.mraw, m.lsem.at[2])
    get_comp = pltpu.make_async_copy(comp.at[0, 0], m.craw, m.lsem.at[3])
    get_fb = pltpu.make_async_copy(fb.at[c], m.fbs, m.lsem.at[4])
    get_er = pltpu.make_async_copy(er.at[c], m.ers.at[0], m.lsem.at[5])
    get_er_low = pltpu.make_async_copy(er.at[jnp.maximum(c - 1, 0)], m.ers.at[1], m.lsem.at[6])
    for copy in (get_fb, get_er, get_er_low, get_loads, get_modes, get_cinv, get_comp):
        copy.start()

    barrier = pltpu.get_barrier_semaphore()
    wide = sorted(
        ((dc, dx) for dc in range(nc) for dx in range(nx) if dc or dx),
        key=lambda d: -min(d[0], nc - d[0]) - 2 * min(d[1], nx - d[1]),
    )
    greeted = [z_peer(step) for step in range(1, nz)] + [cx_peer(d) for d in wide] + [beside[0], beside[1]]
    for peer in greeted:
        pl.semaphore_signal(barrier, inc=1, device_id=peer, device_id_type=pl.DeviceIdType.MESH)

    for copy in (get_fb, get_er, get_er_low):
        copy.wait()
    faces = [m.fbs[f, s] for f in range(4)]
    rank = jnp.int32(0)
    place = [jnp.int32(0)] * NBLOCKS
    pick = [[] for _ in range(NBLOCKS)]
    for b in range(NBLOCKS):
        hits = [same(face, b) for face in faces]
        free = 1 - (hits[0] + hits[1] + hits[2] + hits[3])
        hits = hits + [free * same(rank, j) for j in range(4)]
        for p in range(NBLOCKS):
            pick[p].append(hits[p].astype(F32))
            place[p] = place[p] + b * hits[p]
        rank = rank + free

    def gathered(p, parts):
        value = pick[p][0] * parts[0]
        for b in range(1, NBLOCKS):
            value = value + pick[p][b] * parts[b]
        return value

    for p in range(NBLOCKS):
        place_out[p] = place[p]

    shared = [
        m.ers[0, 0, jnp.maximum(s - 1, 0)] * jnp.minimum(s, 1),
        m.ers[0, 0, s] * jnp.minimum(ns - 1 - s, 1),
        m.ers[1, 1, s] * jnp.minimum(c, 1),
        m.ers[0, 1, s] * jnp.minimum(nc - 1 - c, 1),
    ]
    row_at = lax.broadcasted_iota(jnp.int32, (BLOCK, width), 0)
    for f in range(4):
        m.weight[pl.ds(f * BLOCK, BLOCK), :] = 0.5 * jnp.clip(shared[f] - row_at, 0, 1).astype(F32)

    def halved(face, value):
        return m.weight[pl.ds(face * BLOCK, BLOCK), :] * value

    def rows(p):
        return pl.ds(p * BLOCK, BLOCK)

    def loop_rows(first, count, body):
        def step(i, carry):
            body(pl.ds(pl.multiple_of(first + i * CHUNK, CHUNK), CHUNK))
            return carry
        lax.fori_loop(0, count // CHUNK, step, 0)

    def to_halves(source):
        def body(at):
            high, low = split(source[at, :])
            m.vhi[at, :] = high
            m.vlo[at, :] = low
        return body

    get_modes.wait()
    high, low = split(m.braw[...])
    m.bhl[0:MODES, :] = high
    m.bhl[MODES:2 * MODES, :] = low
    get_loads.wait()
    loop_rows(0, ORDER, to_halves(m.raw))

    def coarse(first, count):
        ks = pl.ds(first, count)
        both = mm(m.bhl[:, ks], m.vhi[ks, :])
        return both[:MODES] + both[MODES:] + mm(m.bhl[0:MODES, ks], m.vlo[ks, :])

    pending = []

    def send(src, dst, send_sem, recv_sem, device):
        copy = remote(src, dst, send_sem, recv_sem, device)
        copy.start()
        pending.append(copy)

    far_first = sorted(range(1, nz), key=lambda step: -min(step, nz - step))

    early = MODES // 2

    def z_gather_start(k):
        for step in (2, nz - 2, 1, nz - 1):
            mine = m.zg.at[k, zm]
            send(mine, mine, m.zss.at[k, step], m.zrs.at[k, step], z_peer(step))

    def z_wait(k, step, sem, first=0, count=MODES):
        slot = m.zg.at[k, z_at(-step), pl.ds(first, count), :]
        remote(slot, slot, m.zss.at[k, sem], m.zrs.at[k, sem], z_peer(step)).wait_recv()

    def z_gather_forward(k):
        for sign, first, count, sem in ((1, 0, early, 4), (-1, early, MODES - early, nz)):
            z_wait(k, 2 * sign, (2 * sign) % nz)
            slot = m.zg.at[k, z_at(-2 * sign)]
            step = (3 * sign) % nz
            send(slot, slot, m.zss.at[k, step], m.zrs.at[k, step], z_peer(sign))
            slot = m.zg.at[k, z_at(-2 * sign), pl.ds(first, count), :]
            send(slot, slot, m.zss.at[k, sem], m.zrs.at[k, sem], z_peer(2 * sign))

    def z_sums(k, value):
        m.dz[k, zm] = value
        for step in far_first:
            mine = m.dz.at[k, zm]
            send(mine, mine, m.dzs.at[k, step], m.dzr.at[k, step], z_peer(step))

    def z_sums_total(k):
        for step in reversed(far_first):
            slot = m.dz.at[k, z_at(-step)]
            remote(slot, slot, m.dzs.at[k, step], m.dzr.at[k, step], z_peer(step)).wait_recv()
        total = m.dz[k, 0]
        for j in range(1, nz):
            total = total + m.dz[k, j]
        return total

    def z_gather_wait(k):
        for step in (1, -1, 3, -3):
            z_wait(k, step, step % nz)
        z_wait(k, 4, 4, 0, early)
        z_wait(k, 4, nz, early, MODES - early)

    m.zg[0, zm] = coarse(0, ORDER)
    pl.semaphore_wait(barrier, len(greeted))
    z_gather_start(0)

    get_cinv.wait()
    span = nz * MODES
    for step in range(1, nx):
        src = m.mraw.at[:, pl.ds(pl.multiple_of(x_at(step) * span, BLOCK), span)]
        send(src, m.mt.at[xm], m.mss.at[step], m.mrs.at[step], x_peer(step))
    m.mt[xm] = m.mraw[:, pl.ds(pl.multiple_of(xm * span, BLOCK), span)]
    for k in range(ITERS):
        m.xs[k, :, MODES:PACK, :] = jnp.zeros((nx, PACK - MODES, width), F32)
    modes_at = [m.braw[:, rows(b)] for b in range(NBLOCKS)]
    for p in range(NBLOCKS):
        part = gathered(p, modes_at)
        high, low = split(part)
        m.bhl[0:MODES, rows(p)] = high
        m.bhl[MODES:2 * MODES, rows(p)] = low
        if p < 4:
            m.bfs[p] = part
    for f in range(4):
        send(m.bfs.at[f], m.bfr.at[f ^ 1], m.bss.at[f], m.brs.at[f ^ 1], beside[f])

    def in_blocks(i, carry):
        parts = [m.raw[pl.ds(pl.multiple_of(b * BLOCK + i * 8, 8), 8), :] for b in range(NBLOCKS)]
        for p in range(NBLOCKS):
            m.r[pl.ds(pl.multiple_of(p * BLOCK + i * 8, 8), 8), :] = gathered(p, parts)
        return carry

    def columns_in_order(i, carry):
        at = pl.ds(pl.multiple_of(i * 16, 16), 16)
        parts = [m.craw[at, rows(b)] for b in range(NBLOCKS)]
        values = [gathered(q, parts) for q in range(NBLOCKS)]
        for q in range(NBLOCKS):
            m.craw[at, rows(q)] = values[q]
        return carry

    def rows_in_order(i, carry):
        for q in range(NBLOCKS):
            parts = [m.craw[pl.ds(pl.multiple_of(b * BLOCK + i * 16, 16), 16), rows(q)] for b in range(NBLOCKS)]
            for p in range(NBLOCKS):
                at = pl.ds(pl.multiple_of(p * BLOCK + i * 16, 16), 16)
                high, low = split(gathered(p, parts))
                m.chi[at, rows(q)] = high
                m.clo[at, rows(q)] = low
        return carry

    lax.fori_loop(0, BLOCK // 8, in_blocks, 0)
    get_comp.wait()
    lax.fori_loop(0, ORDER // 16, columns_in_order, 0)
    z_gather_forward(0)
    for f in range(4):
        remote(m.r.at[rows(f), :], m.rp.at[rows(f ^ 1), :], m.rss.at[f], m.rrs.at[f ^ 1], beside[f]).start()

    def transposed(high, low):
        stacked = jnp.concatenate([high.astype(F32), low.astype(F32), high.astype(F32), jnp.zeros((MODES, BLOCK), F32)], axis=0)
        return stacked.T.astype(BF16)

    for p in range(NBLOCKS):
        m.bt[rows(p), :] = transposed(m.bhl[0:MODES, rows(p)], m.bhl[MODES:2 * MODES, rows(p)])
    m.yk[:, 3 * MODES:, :] = jnp.zeros((5, MODES, width), BF16)
    lax.fori_loop(0, BLOCK // 16, rows_in_order, 0)

    for step in range(1, nx):
        slot = m.mt.at[x_at(-step)]
        remote(slot, slot, m.mss.at[step], m.mrs.at[step], x_peer(step)).wait_recv()
    high, low = split(m.mt[...].reshape(nx * MODES, span))
    m.mhl[0:nx * MODES, :] = high
    m.mhl[nx * MODES:, :] = low
    for f in range(4):
        slot = m.bfr.at[f]
        remote(slot, slot, m.bss.at[f], m.brs.at[f], beside[f]).wait_recv()
        m.bpt[rows(f), :] = transposed(*split(m.bfr[f]))

    def stack_y(i, value):
        high, low = split(value)
        m.yk[i, 0:MODES, :] = high
        m.yk[i, MODES:2 * MODES, :] = high
        m.yk[i, 2 * MODES:3 * MODES, :] = low

    def solve_coarse(k):
        z_gather_wait(k)
        high, low = split(m.zg[k].reshape(nz * MODES, width))
        both = mm(m.mhl[...], high)
        half = nx * MODES
        part = both[:half] + both[half:] + mm(m.mhl[0:half, :], low)
        m.xs[k, :, 0:MODES, :] = part.reshape(nx, MODES, width)
        if k > 0:
            sums = z_sums_total(k)
            for j in range(nx):
                m.xs[k, j, MODES:MODES + SUMS, :] = sums
        for step in range(1, nx):
            send(m.xs.at[k, x_at(step)], m.xr.at[k, xm], m.xss.at[k, step], m.xrs.at[k, step], x_peer(step))
        m.xr[k, xm] = m.xs[k, xm]
        for step in range(1, nx):
            slot = m.xr.at[k, x_at(-step)]
            remote(slot, slot, m.xss.at[k, step], m.xrs.at[k, step], x_peer(step)).wait_recv()
        total = m.xr[k, 0]
        for j in range(1, nx):
            total = total + m.xr[k, j]
        m.yo[k] = total[:MODES]
        for f in range(4):
            send(m.yo.at[k], m.yp.at[k, f ^ 1], m.yss.at[k, f], m.yrs.at[k, f ^ 1], beside[f])
        stack_y(4, total[:MODES])
        return total[MODES:MODES + SUMS]

    def wait_y(k, f):
        slot = m.yp.at[k, f]
        remote(slot, slot, m.yss.at[k, f], m.yrs.at[k, f], beside[f]).wait_recv()

    def product(at, ks):
        return mm(m.chi[at, ks], m.vhi[ks, :]) + mm(m.chi[at, ks], m.vlo[ks, :]) + mm(m.clo[at, ks], m.vhi[ks, :])

    def keep_halves(at, value):
        high, low = split(value)
        m.vhi[at, :] = high
        m.vlo[at, :] = low

    near, inside = pl.ds(0, FACE_ROWS), pl.ds(FACE_ROWS, ORDER - FACE_ROWS)
    near_parts = [pl.ds(i, WIDE) for i in range(0, FACE_ROWS, WIDE)]
    inside_parts = [pl.ds(i, WIDE) for i in range(FACE_ROWS, ORDER, WIDE)]

    def coefficients(sums, old):
        rz, curve = sums[0:1], sums[1:2]
        if old is None:
            return rz, None, rz / curve
        ratio = rz / old[0]
        return rz, ratio, rz / (curve - ratio * rz / old[2])

    solve_coarse(0)
    coeff = None
    for k in range(ITERS):
        z = m.z.at[k]
        t = m.t.at[k]
        if k > 0:
            w = m.t.at[k - 1]
            z_old = m.z.at[k - 1]
            _, ratio, alpha = coeff
        for at in inside_parts + near_parts:
            value = mm(m.bt[at, :], m.yk[4])
            if k == 0:
                value = m.r[at, :] + value
            else:
                value = w[at, :] + value
                if ratio is not None:
                    value = value + ratio * m.q[at, :]
                m.q[at, :] = value
                value = z_old[at, :] - alpha * value
            z[at, :] = value
            if at in inside_parts:
                keep_halves(at, value)
        for at in near_parts + inside_parts:
            t[at, :] = product(at, inside)
        def update(i, total, z=z):
            at = pl.ds(pl.multiple_of(i * CHUNK, CHUNK), CHUNK)
            r = m.r[at, :]
            if k > 0:
                s_new, d_new = w[at, :], z_old[at, :]
                if ratio is not None:
                    s_new = s_new + ratio * m.s[at, :]
                    d_new = d_new + ratio * m.d[at, :]
                m.s[at, :] = s_new
                m.d[at, :] = d_new
                m.x[at, :] = alpha * d_new if k == 1 else m.x[at, :] + alpha * d_new
                r = r - alpha * s_new
                m.r[at, :] = r
            return total + fold(r * z[at, :])
        zero = jnp.zeros((8, width), F32)
        first = lax.fori_loop(0, ORDER // CHUNK, update, zero)
        m.own[k, 0:1, :] = jnp.sum(first, axis=0, keepdims=True)
        for f in (2, 3, 0, 1):
            wait_y(k, f)
            if k == 0:
                slot = m.rp.at[rows(f), :]
                copy = remote(slot, slot, m.rss.at[f], m.rrs.at[f], beside[f])
                copy.wait_recv()
                copy.wait_send()
        for f in range(4):
            stack_y(f, m.yp[k, f])
        for f in range(4):
            value = mm(m.bpt[rows(f), :], m.yk[f])
            if k == 0:
                value = m.rp[rows(f), :] + value
            else:
                value = m.wp[rows(f), :] + value
                if ratio is not None:
                    value = value + ratio * m.qp[rows(f), :]
                m.qp[rows(f), :] = value
                value = m.zp[rows(f), :] - alpha * value
            m.zp[rows(f), :] = value
            inner = z[rows(f), :] + halved(f, value)
            m.inner[rows(f), :] = inner
            keep_halves(rows(f), inner)
        for f in range(4):
            m.ts[k, rows(f), :] = t[rows(f), :] + product(rows(f), near)
            send(m.ts.at[k, rows(f), :], m.tp.at[k, rows(f ^ 1), :], m.tss.at[k, f], m.trs.at[k, f ^ 1], beside[f])
        for at in inside_parts:
            value = t[at, :] + product(at, near)
            t[at, :] = value
            if k + 1 < ITERS:
                keep_halves(at, value)

        def dots(i, total, z=z, t=t, k=k):
            at = pl.ds(pl.multiple_of(i * CHUNK, CHUNK), CHUNK)
            low_at = pl.ds(pl.multiple_of(FACE_ROWS + i * CHUNK, CHUNK), CHUNK)
            return total + fold(m.inner[at, :] * m.ts[k, at, :]) + fold(z[low_at, :] * t[low_at, :])
        second = lax.fori_loop(0, FACE_ROWS // CHUNK, dots, zero)
        m.own[k, 1:2, :] = jnp.sum(second, axis=0, keepdims=True)
        if k + 1 < ITERS:
            m.cd[k, c] = m.own[k]
            for step in range(1, nc):
                mine = m.cd.at[k, c]
                send(mine, mine, m.css.at[k, step], m.crs.at[k, step], c_peer(step))
        else:
            m.fd[c, xm] = m.own[k]
            for dc, dx in wide:
                mine = m.fd.at[c, xm]
                send(mine, mine, m.fss.at[dc, dx], m.frs.at[dc, dx], cx_peer((dc, dx)))
        if k + 1 < ITERS:
            part = coarse(FACE_ROWS, ORDER - FACE_ROWS)
        for f in range(4):
            slot = m.tp.at[k, rows(f), :]
            remote(slot, slot, m.tss.at[k, f], m.trs.at[k, f], beside[f]).wait_recv()
        for f in range(4):
            own = m.ts[k, rows(f), :]
            theirs = m.tp[k, rows(f), :]
            value = own + halved(f, theirs)
            t[rows(f), :] = value
            if k + 1 < ITERS:
                m.wp[rows(f), :] = theirs + halved(f, own)
                keep_halves(rows(f), value)
        if k + 1 < ITERS:
            part = part + coarse(0, FACE_ROWS)
        if k + 1 < ITERS:
            m.zg[k + 1, zm] = part
            z_gather_start(k + 1)
            for step in range(1, nc):
                slot = m.cd.at[k, c_at(-step)]
                remote(slot, slot, m.css.at[k, step], m.crs.at[k, step], c_peer(step)).wait_recv()
            sums = m.cd[k, 0]
            for j in range(1, nc):
                sums = sums + m.cd[k, j]
            z_sums(k + 1, sums)
            z_gather_forward(k + 1)
            coeff = coefficients(solve_coarse(k + 1), coeff)

    for dc, dx in reversed(wide):
        slot = m.fd.at[c_at(-dc), x_at(-dx)]
        remote(slot, slot, m.fss.at[dc, dx], m.frs.at[dc, dx], cx_peer((dc, dx))).wait_recv()
    sums = m.fd[0, 0]
    for i in range(nc):
        for j in range(nx):
            if i or j:
                sums = sums + m.fd[i, j]
    z_sums(0, sums)
    sums = z_sums_total(0)
    _, ratio, alpha = coefficients(sums, coeff)
    z = m.z.at[ITERS - 1]
    t = m.t.at[ITERS - 1]

    def finish(at):
        m.out[0, at, :] = m.x[at, :] + alpha * (z[at, :] + ratio * m.d[at, :])
        m.out[1, at, :] = m.r[at, :] - alpha * (t[at, :] + ratio * m.s[at, :])
    half = ORDER // 2
    outs = []
    for i in range(2):
        loop_rows(i * half, half, finish)
        at = pl.ds(i * half, half)
        for j, into in enumerate((x_out, r_out)):
            outs.append(pltpu.make_async_copy(m.out.at[j, at, :], into.at[0, 0, at, :], m.lsem.at[2 * i + j]))
            outs[-1].start()
    for copy in outs:
        copy.wait()
    for copy in pending:
        copy.wait_send()


class Names:
    def __init__(self, names, refs):
        for name, ref in zip(names, refs, strict=True):
            setattr(self, name, ref)


def scratch(nx, nz, nc, width):
    vmem, dma = pltpu.VMEM, pltpu.SemaphoreType.DMA
    span = nz * MODES
    full, face = (ORDER, width), (FACE_ROWS, width)
    return dict(
        raw=vmem(full, F32), braw=vmem((MODES, ORDER), F32), mraw=vmem((MODES, nx * span), F32), craw=vmem((ORDER, ORDER), F32),
        fbs=pltpu.SMEM((4, nx * nz), jnp.int32), ers=pltpu.SMEM((2, 2, nx * nz), jnp.int32),
        chi=vmem((ORDER, ORDER), BF16), clo=vmem((ORDER, ORDER), BF16), vhi=vmem(full, BF16), vlo=vmem(full, BF16),
        bhl=vmem((2 * MODES, ORDER), BF16), bt=vmem((ORDER, BLOCK), BF16), bpt=vmem((FACE_ROWS, BLOCK), BF16),
        yk=vmem((5, BLOCK, width), BF16), mt=vmem((nx, MODES, span), F32), mhl=vmem((2 * nx * MODES, span), BF16),
        zg=vmem((ITERS, nz, MODES, width), F32), xs=vmem((ITERS, nx, PACK, width), F32), xr=vmem((ITERS, nx, PACK, width), F32),
        yo=vmem((ITERS, MODES, width), F32), yp=vmem((ITERS, 4, MODES, width), F32),
        ts=vmem((ITERS, *face), F32), tp=vmem((ITERS, *face), F32), cd=vmem((ITERS, nc, SUMS, width), F32),
        own=vmem((ITERS, SUMS, width), F32), dz=vmem((ITERS, nz, SUMS, width), F32), fd=vmem((nc, nx, SUMS, width), F32),
        bfs=vmem((4, MODES, BLOCK), F32), bfr=vmem((4, MODES, BLOCK), F32), rp=vmem(face, F32),
        z=vmem((ITERS, *full), F32), t=vmem((ITERS, *full), F32), q=vmem(full, F32), s=vmem(full, F32), r=vmem(full, F32),
        d=vmem(full, F32), x=vmem(full, F32), zp=vmem(face, F32), qp=vmem(face, F32), wp=vmem(face, F32), inner=vmem(face, F32), weight=vmem(face, F32), out=vmem((2, *full), F32),
        lsem=dma((8,)), zss=dma((ITERS, nz + 1)), zrs=dma((ITERS, nz + 1)), xss=dma((ITERS, nx)), xrs=dma((ITERS, nx)),
        yss=dma((ITERS, 4)), yrs=dma((ITERS, 4)), tss=dma((ITERS, 4)), trs=dma((ITERS, 4)), css=dma((ITERS, nc)), crs=dma((ITERS, nc)),
        dzs=dma((ITERS, nz)), dzr=dma((ITERS, nz)), fss=dma((nc, nx)), frs=dma((nc, nx)), mss=dma((nx,)), mrs=dma((nx,)),
        bss=dma((4,)), brs=dma((4,)), rss=dma((4,)), rrs=dma((4,)),
    )


def back_in_place(place, x, r, x_out, r_out, held, get, put):
    pairs = [(p, j) for p in range(NBLOCKS) for j in range(2)]
    sources, intos = (x, r), (x_out, r_out)

    def load(p, j):
        at = pl.ds(p * BLOCK, BLOCK)
        return pltpu.make_async_copy(sources[j].at[0, 0, at, :], held.at[j, at, :], get.at[j, p])

    def store(p, j):
        at = pl.ds(pl.multiple_of(place[p] * BLOCK, BLOCK), BLOCK)
        return pltpu.make_async_copy(held.at[j, pl.ds(p * BLOCK, BLOCK), :], intos[j].at[0, 0, at, :], put.at[j, p])

    for p, j in pairs:
        load(p, j).start()
    for p, j in pairs:
        load(p, j).wait()
        store(p, j).start()
    for p, j in pairs:
        store(p, j).wait()


def shards(nx, nz, nc, compliance, loads, modes, coarse_inverse, face_block, edge_rows):
    width = loads.shape[-1]
    held = scratch(nx, nz, nc, width)

    def body(*refs):
        kernel(nx, nz, nc, *refs[:9], Names(held, refs[9:]))

    anywhere = pl.BlockSpec(memory_space=pl.ANY)
    small = pl.BlockSpec(memory_space=pltpu.SMEM)
    shapes = [jax.ShapeDtypeStruct(loads.shape, F32)] * 2
    x, r, place = pl.pallas_call(
        body,
        out_shape=shapes + [jax.ShapeDtypeStruct((NBLOCKS,), jnp.int32)],
        in_specs=[anywhere] * 6,
        out_specs=[anywhere, anywhere, small],
        scratch_shapes=list(held.values()),
        compiler_params=pltpu.CompilerParams(collective_id=0, has_side_effects=True, vmem_limit_bytes=56 * 1024 * 1024),
    )(compliance, loads, modes, coarse_inverse, jnp.transpose(face_block, (0, 2, 1)), jnp.transpose(edge_rows, (0, 2, 1)))
    return pl.pallas_call(
        back_in_place,
        out_shape=shapes,
        in_specs=[small, anywhere, anywhere],
        out_specs=[anywhere, anywhere],
        scratch_shapes=[pltpu.VMEM((2, ORDER, width), F32)] + [pltpu.SemaphoreType.DMA((2, NBLOCKS))] * 2,
    )(place, x, r)


def solution(mesh, nz=NZ):
    nc, ns = mesh.shape["cluster"], mesh.shape["sub"]
    cut = P("cluster", "sub", None, None)
    return jax.shard_map(
        functools.partial(shards, ns // nz, nz, nc), mesh=mesh,
        in_specs=(cut, cut, cut, P("cluster", "sub", None), P(), P()),
        out_specs=(cut, cut), check_vma=False,
    )
```

```python
import functools

import jax
import jax.numpy as jnp
from jax import lax
from jax.experimental import pallas as pl
from jax.experimental.pallas import tpu as pltpu
from jax.sharding import PartitionSpec as P

BLOCK = 128
NBLOCKS = 8
ORDER = BLOCK * NBLOCKS
FACE_ROWS = 4 * BLOCK
MODES = 32
SUMS = 2
PACK = MODES + 8
ITERS = 3
NZ = 8
CHUNK = 64
WIDE = 256
F32 = jnp.float32
BF16 = jnp.bfloat16


def split(value):
    high = value.astype(BF16)
    return high, (value - high.astype(F32)).astype(BF16)


def mm(left, right):
    return jnp.dot(left, right, preferred_element_type=F32)


def same(left, right):
    gap = left - right
    return 1 - jnp.minimum(gap * gap, 1)


def fold(value):
    rows, width = value.shape
    return jnp.sum(value.reshape(rows // 8, 8, width), axis=0)


def remote(src, dst, send_sem, recv_sem, device):
    return pltpu.make_async_remote_copy(
        src_ref=src, dst_ref=dst, send_sem=send_sem, recv_sem=recv_sem,
        device_id=device, device_id_type=pl.DeviceIdType.MESH,
    )


def kernel(nx, nz, nc, comp, loads, modes, cinv, fb, er, x_out, r_out, place_out, m):
    ns = nx * nz
    c = lax.axis_index("cluster")
    s = lax.axis_index("sub")
    xm = lax.div(s, nz)
    zm = lax.rem(s, nz)
    width = m.raw.shape[1]

    def z_at(step):
        return lax.rem(zm + (step + nz), nz)

    def x_at(step):
        return lax.rem(xm + (step + nx), nx)

    def c_at(step):
        return lax.rem(c + (step + nc), nc)

    def z_peer(step):
        return (c, xm * nz + z_at(step))

    def x_peer(step):
        return (c, x_at(step) * nz + zm)

    def c_peer(step):
        return (c_at(step), s)

    def cx_peer(step):
        return (c_at(step[0]), x_at(step[1]) * nz + zm)

    beside = (
        (c, lax.rem(s + ns - 1, ns)),
        (c, lax.rem(s + 1, ns)),
        (c_at(-1), s),
        (c_at(1), s),
    )

    get_loads = pltpu.make_async_copy(loads.at[0, 0], m.raw, m.lsem.at[0])
    get_modes = pltpu.make_async_copy(modes.at[0, 0], m.braw, m.lsem.at[1])
    get_cinv = pltpu.make_async_copy(cinv.at[0], m.mraw, m.lsem.at[2])
    get_comp = pltpu.make_async_copy(comp.at[0, 0], m.craw, m.lsem.at[3])
    get_fb = pltpu.make_async_copy(fb.at[c], m.fbs, m.lsem.at[4])
    get_er = pltpu.make_async_copy(er.at[c], m.ers.at[0], m.lsem.at[5])
    get_er_low = pltpu.make_async_copy(er.at[jnp.maximum(c - 1, 0)], m.ers.at[1], m.lsem.at[6])
    for copy in (get_fb, get_er, get_er_low, get_loads, get_modes, get_cinv, get_comp):
        copy.start()

    barrier = pltpu.get_barrier_semaphore()
    wide = sorted(
        ((dc, dx) for dc in range(nc) for dx in range(nx) if dc or dx),
        key=lambda d: -min(d[0], nc - d[0]) - 2 * min(d[1], nx - d[1]),
    )
    greeted = [z_peer(step) for step in range(1, nz)] + [cx_peer(d) for d in wide] + [beside[0], beside[1]]
    for peer in greeted:
        pl.semaphore_signal(barrier, inc=1, device_id=peer, device_id_type=pl.DeviceIdType.MESH)

    for copy in (get_fb, get_er, get_er_low):
        copy.wait()
    faces = [m.fbs[f, s] for f in range(4)]
    rank = jnp.int32(0)
    place = [jnp.int32(0)] * NBLOCKS
    pick = [[] for _ in range(NBLOCKS)]
    for b in range(NBLOCKS):
        hits = [same(face, b) for face in faces]
        free = 1 - (hits[0] + hits[1] + hits[2] + hits[3])
        hits = hits + [free * same(rank, j) for j in range(4)]
        for p in range(NBLOCKS):
            pick[p].append(hits[p].astype(F32))
            place[p] = place[p] + b * hits[p]
        rank = rank + free

    def gathered(p, parts):
        value = pick[p][0] * parts[0]
        for b in range(1, NBLOCKS):
            value = value + pick[p][b] * parts[b]
        return value

    for p in range(NBLOCKS):
        place_out[p] = place[p]

    shared = [
        m.ers[0, 0, jnp.maximum(s - 1, 0)] * jnp.minimum(s, 1),
        m.ers[0, 0, s] * jnp.minimum(ns - 1 - s, 1),
        m.ers[1, 1, s] * jnp.minimum(c, 1),
        m.ers[0, 1, s] * jnp.minimum(nc - 1 - c, 1),
    ]
    row_at = lax.broadcasted_iota(jnp.int32, (BLOCK, width), 0)
    for f in range(4):
        m.weight[pl.ds(f * BLOCK, BLOCK), :] = 0.5 * jnp.clip(shared[f] - row_at, 0, 1).astype(F32)

    def halved(face, value):
        return m.weight[pl.ds(face * BLOCK, BLOCK), :] * value

    def rows(p):
        return pl.ds(p * BLOCK, BLOCK)

    def loop_rows(first, count, body):
        def step(i, carry):
            body(pl.ds(pl.multiple_of(first + i * CHUNK, CHUNK), CHUNK))
            return carry
        lax.fori_loop(0, count // CHUNK, step, 0)

    def to_halves(source):
        def body(at):
            high, low = split(source[at, :])
            m.vhi[at, :] = high
            m.vlo[at, :] = low
        return body

    get_modes.wait()
    high, low = split(m.braw[...])
    m.bhl[0:MODES, :] = high
    m.bhl[MODES:2 * MODES, :] = low
    get_loads.wait()
    loop_rows(0, ORDER, to_halves(m.raw))

    def coarse(first, count):
        ks = pl.ds(first, count)
        both = mm(m.bhl[:, ks], m.vhi[ks, :])
        return both[:MODES] + both[MODES:] + mm(m.bhl[0:MODES, ks], m.vlo[ks, :])

    pending = []

    def send(src, dst, send_sem, recv_sem, device):
        copy = remote(src, dst, send_sem, recv_sem, device)
        copy.start()
        pending.append(copy)

    far_first = sorted(range(1, nz), key=lambda step: -min(step, nz - step))

    early = MODES // 2

    def z_gather_start(k):
        for step in (2, nz - 2, 1, nz - 1):
            mine = m.zg.at[k, zm]
            send(mine, mine, m.zss.at[k, step], m.zrs.at[k, step], z_peer(step))

    def z_wait(k, step, sem, first=0, count=MODES):
        slot = m.zg.at[k, z_at(-step), pl.ds(first, count), :]
        remote(slot, slot, m.zss.at[k, sem], m.zrs.at[k, sem], z_peer(step)).wait_recv()

    def z_gather_forward(k):
        for sign, first, count, sem in ((1, 0, early, 4), (-1, early, MODES - early, nz)):
            z_wait(k, 2 * sign, (2 * sign) % nz)
            slot = m.zg.at[k, z_at(-2 * sign)]
            step = (3 * sign) % nz
            send(slot, slot, m.zss.at[k, step], m.zrs.at[k, step], z_peer(sign))
            slot = m.zg.at[k, z_at(-2 * sign), pl.ds(first, count), :]
            send(slot, slot, m.zss.at[k, sem], m.zrs.at[k, sem], z_peer(2 * sign))

    def z_sums(k, value):
        m.dz[k, zm] = value
        for step in far_first:
            mine = m.dz.at[k, zm]
            send(mine, mine, m.dzs.at[k, step], m.dzr.at[k, step], z_peer(step))

    def z_sums_total(k):
        for step in reversed(far_first):
            slot = m.dz.at[k, z_at(-step)]
            remote(slot, slot, m.dzs.at[k, step], m.dzr.at[k, step], z_peer(step)).wait_recv()
        total = m.dz[k, 0]
        for j in range(1, nz):
            total = total + m.dz[k, j]
        return total

    def z_gather_wait(k):
        for step in (1, -1, 3, -3):
            z_wait(k, step, step % nz)
        z_wait(k, 4, 4, 0, early)
        z_wait(k, 4, nz, early, MODES - early)

    m.zg[0, zm] = coarse(0, ORDER)
    pl.semaphore_wait(barrier, len(greeted))
    z_gather_start(0)

    get_cinv.wait()
    span = nz * MODES
    for step in range(1, nx):
        src = m.mraw.at[:, pl.ds(pl.multiple_of(x_at(step) * span, BLOCK), span)]
        send(src, m.mt.at[xm], m.mss.at[step], m.mrs.at[step], x_peer(step))
    m.mt[xm] = m.mraw[:, pl.ds(pl.multiple_of(xm * span, BLOCK), span)]
    for k in range(ITERS):
        m.xs[k, :, MODES:PACK, :] = jnp.zeros((nx, PACK - MODES, width), F32)
    modes_at = [m.braw[:, rows(b)] for b in range(NBLOCKS)]
    for p in range(NBLOCKS):
        part = gathered(p, modes_at)
        high, low = split(part)
        m.bhl[0:MODES, rows(p)] = high
        m.bhl[MODES:2 * MODES, rows(p)] = low
        if p < 4:
            m.bfs[p] = part
    for f in range(4):
        send(m.bfs.at[f], m.bfr.at[f ^ 1], m.bss.at[f], m.brs.at[f ^ 1], beside[f])

    def in_blocks(i, carry):
        parts = [m.raw[pl.ds(pl.multiple_of(b * BLOCK + i * 8, 8), 8), :] for b in range(NBLOCKS)]
        for p in range(NBLOCKS):
            m.r[pl.ds(pl.multiple_of(p * BLOCK + i * 8, 8), 8), :] = gathered(p, parts)
        return carry

    def columns_in_order(i, carry):
        at = pl.ds(pl.multiple_of(i * 16, 16), 16)
        parts = [m.craw[at, rows(b)] for b in range(NBLOCKS)]
        values = [gathered(q, parts) for q in range(NBLOCKS)]
        for q in range(NBLOCKS):
            m.craw[at, rows(q)] = values[q]
        return carry

    def rows_in_order(i, carry):
        for q in range(NBLOCKS):
            parts = [m.craw[pl.ds(pl.multiple_of(b * BLOCK + i * 16, 16), 16), rows(q)] for b in range(NBLOCKS)]
            for p in range(NBLOCKS):
                at = pl.ds(pl.multiple_of(p * BLOCK + i * 16, 16), 16)
                high, low = split(gathered(p, parts))
                m.chi[at, rows(q)] = high
                m.clo[at, rows(q)] = low
        return carry

    lax.fori_loop(0, BLOCK // 8, in_blocks, 0)
    get_comp.wait()
    lax.fori_loop(0, ORDER // 16, columns_in_order, 0)
    z_gather_forward(0)
    for f in range(4):
        remote(m.r.at[rows(f), :], m.rp.at[rows(f ^ 1), :], m.rss.at[f], m.rrs.at[f ^ 1], beside[f]).start()

    def transposed(high, low):
        stacked = jnp.concatenate([high.astype(F32), low.astype(F32), high.astype(F32), jnp.zeros((MODES, BLOCK), F32)], axis=0)
        return stacked.T.astype(BF16)

    for p in range(NBLOCKS):
        m.bt[rows(p), :] = transposed(m.bhl[0:MODES, rows(p)], m.bhl[MODES:2 * MODES, rows(p)])
    m.yk[:, 3 * MODES:, :] = jnp.zeros((5, MODES, width), BF16)
    lax.fori_loop(0, BLOCK // 16, rows_in_order, 0)

    for step in range(1, nx):
        slot = m.mt.at[x_at(-step)]
        remote(slot, slot, m.mss.at[step], m.mrs.at[step], x_peer(step)).wait_recv()
    high, low = split(m.mt[...].reshape(nx * MODES, span))
    m.mhl[0:nx * MODES, :] = high
    m.mhl[nx * MODES:, :] = low
    for f in range(4):
        slot = m.bfr.at[f]
        remote(slot, slot, m.bss.at[f], m.brs.at[f], beside[f]).wait_recv()
        high, low = split(m.bfr[f])
        m.bpt[rows(f), :] = transposed(high, low)
        m.bph[f, 0:MODES, :] = high
        m.bph[f, MODES:2 * MODES, :] = low

    def stack_y(i, value):
        high, low = split(value)
        m.yk[i, 0:MODES, :] = high
        m.yk[i, MODES:2 * MODES, :] = high
        m.yk[i, 2 * MODES:3 * MODES, :] = low

    def send_faces(k):
        for f in range(4):
            send(m.ts.at[k, rows(f), :], m.tp.at[k, rows(f ^ 1), :], m.tss.at[k, f], m.trs.at[k, f ^ 1], beside[f])

    def image_on_faces(k):
        for f in range(4):
            slot = m.tp.at[k, rows(f), :]
            remote(slot, slot, m.tss.at[k, f], m.trs.at[k, f], beside[f]).wait_recv()
        for f in range(4):
            own = m.ts[k, rows(f), :]
            theirs = m.tp[k, rows(f), :]
            m.t[k, rows(f), :] = own + halved(f, theirs)
            if k + 1 < ITERS:
                m.wp[rows(f), :] = theirs + halved(f, own)

    def solve_coarse(k):
        z_gather_wait(k)
        high, low = split(m.zg[k].reshape(nz * MODES, width))
        both = mm(m.mhl[...], high)
        half = nx * MODES
        part = both[:half] + both[half:] + mm(m.mhl[0:half, :], low)
        m.xs[k, :, 0:MODES, :] = part.reshape(nx, MODES, width)
        if k > 0:
            sums = z_sums_total(k)
            for j in range(nx):
                m.xs[k, j, MODES:MODES + SUMS, :] = sums
        for step in range(1, nx):
            send(m.xs.at[k, x_at(step)], m.xr.at[k, xm], m.xss.at[k, step], m.xrs.at[k, step], x_peer(step))
        m.xr[k, xm] = m.xs[k, xm]
        if k > 0:
            send_faces(k - 1)
        for step in range(1, nx):
            slot = m.xr.at[k, x_at(-step)]
            remote(slot, slot, m.xss.at[k, step], m.xrs.at[k, step], x_peer(step)).wait_recv()
        total = m.xr[k, 0]
        for j in range(1, nx):
            total = total + m.xr[k, j]
        m.yo[k] = total[:MODES]
        for f in range(4):
            send(m.yo.at[k], m.yp.at[k, f ^ 1], m.yss.at[k, f], m.yrs.at[k, f ^ 1], beside[f])
        stack_y(4, total[:MODES])
        return total[MODES:MODES + SUMS]

    def wait_y(k, f):
        slot = m.yp.at[k, f]
        remote(slot, slot, m.yss.at[k, f], m.yrs.at[k, f], beside[f]).wait_recv()

    def product(at, ks):
        return mm(m.chi[at, ks], m.vhi[ks, :]) + mm(m.chi[at, ks], m.vlo[ks, :]) + mm(m.clo[at, ks], m.vhi[ks, :])

    def keep_halves(at, value):
        high, low = split(value)
        m.vhi[at, :] = high
        m.vlo[at, :] = low

    near, inside = pl.ds(0, FACE_ROWS), pl.ds(FACE_ROWS, ORDER - FACE_ROWS)
    near_parts = [pl.ds(i, WIDE) for i in range(0, FACE_ROWS, WIDE)]
    inside_parts = [pl.ds(i, WIDE) for i in range(FACE_ROWS, ORDER, WIDE)]

    def coefficients(sums, old):
        rz, curve = sums[0:1], sums[1:2]
        if old is None:
            return rz, None, rz / curve
        ratio = rz / old[0]
        return rz, ratio, rz / (curve - ratio * rz / old[2])

    solve_coarse(0)
    coeff = None
    for k in range(ITERS):
        z = m.z.at[k]
        t = m.t.at[k]
        if k > 0:
            w = m.t.at[k - 1]
            z_old = m.z.at[k - 1]
            _, ratio, alpha = coeff
        def new_z(at):
            value = mm(m.bt[at, :], m.yk[4])
            if k == 0:
                value = m.r[at, :] + value
            else:
                value = w[at, :] + value
                if ratio is not None:
                    value = value + ratio * m.q[at, :]
                m.q[at, :] = value
                value = z_old[at, :] - alpha * value
            z[at, :] = value
            return value
        for at in inside_parts:
            keep_halves(at, new_z(at))
        for at in near_parts + inside_parts:
            t[at, :] = product(at, inside)
        if k > 0:
            image_on_faces(k - 1)
        for at in near_parts:
            new_z(at)
        def update(i, total, z=z):
            at = pl.ds(pl.multiple_of(i * CHUNK, CHUNK), CHUNK)
            r = m.r[at, :]
            if k > 0:
                s_new, d_new = w[at, :], z_old[at, :]
                if ratio is not None:
                    s_new = s_new + ratio * m.s[at, :]
                    d_new = d_new + ratio * m.d[at, :]
                m.s[at, :] = s_new
                m.d[at, :] = d_new
                m.x[at, :] = alpha * d_new if k == 1 else m.x[at, :] + alpha * d_new
                r = r - alpha * s_new
                m.r[at, :] = r
            return total + fold(r * z[at, :])
        zero = jnp.zeros((8, width), F32)
        first = lax.fori_loop(0, ORDER // CHUNK, update, zero)
        m.own[k, 0:1, :] = jnp.sum(first, axis=0, keepdims=True)
        for f in (2, 3, 0, 1):
            wait_y(k, f)
            if k == 0:
                slot = m.rp.at[rows(f), :]
                copy = remote(slot, slot, m.rss.at[f], m.rrs.at[f], beside[f])
                copy.wait_recv()
                copy.wait_send()
        for f in range(4):
            stack_y(f, m.yp[k, f])
        for f in range(4):
            value = mm(m.bpt[rows(f), :], m.yk[f])
            if k == 0:
                value = m.rp[rows(f), :] + value
            else:
                value = m.wp[rows(f), :] + value
                if ratio is not None:
                    value = value + ratio * m.qp[rows(f), :]
                m.qp[rows(f), :] = value
                value = m.zp[rows(f), :] - alpha * value
            m.zp[rows(f), :] = value
            inner = z[rows(f), :] + halved(f, value)
            m.inner[rows(f), :] = inner
            keep_halves(rows(f), inner)
        for f in range(4):
            m.ts[k, rows(f), :] = t[rows(f), :] + product(rows(f), near)
        if k + 1 < ITERS:
            for f in range(4):
                high, low = split(halved(f, m.ts[k, rows(f), :]))
                both = mm(m.bph[f], high)
                m.hs[k, f] = both[:MODES] + both[MODES:] + mm(m.bph[f, 0:MODES, :], low)
                send(m.hs.at[k, f], m.hr.at[k, f ^ 1], m.hss.at[k, f], m.hrs.at[k, f ^ 1], beside[f])
        else:
            send_faces(k)
        def dots(i, total, z=z, t=t, k=k):
            at = pl.ds(pl.multiple_of(i * CHUNK, CHUNK), CHUNK)
            low_at = pl.ds(pl.multiple_of(FACE_ROWS + i * CHUNK, CHUNK), CHUNK)
            return total + fold(m.inner[at, :] * (m.ts[k, at, :] + t[at, :])) + fold(z[low_at, :] * t[low_at, :])
        second = lax.fori_loop(0, FACE_ROWS // CHUNK, dots, zero)
        m.own[k, 1:2, :] = jnp.sum(second, axis=0, keepdims=True)
        if k + 1 < ITERS:
            m.cd[k, c] = m.own[k]
            for step in range(1, nc):
                mine = m.cd.at[k, c]
                send(mine, mine, m.css.at[k, step], m.crs.at[k, step], c_peer(step))
        else:
            m.fd[c, xm] = m.own[k]
            for dc, dx in wide:
                mine = m.fd.at[c, xm]
                send(mine, mine, m.fss.at[dc, dx], m.frs.at[dc, dx], cx_peer((dc, dx)))
        for at in inside_parts:
            value = t[at, :] + product(at, near)
            t[at, :] = value
            if k + 1 < ITERS:
                keep_halves(at, value)

        if k + 1 < ITERS:
            for at in near_parts:
                keep_halves(at, m.ts[k, at, :])
            part = coarse(0, ORDER)
            for f in range(4):
                slot = m.hr.at[k, f]
                remote(slot, slot, m.hss.at[k, f], m.hrs.at[k, f], beside[f]).wait_recv()
                part = part + m.hr[k, f]
            m.zg[k + 1, zm] = part
            z_gather_start(k + 1)
            for step in range(1, nc):
                slot = m.cd.at[k, c_at(-step)]
                remote(slot, slot, m.css.at[k, step], m.crs.at[k, step], c_peer(step)).wait_recv()
            sums = m.cd[k, 0]
            for j in range(1, nc):
                sums = sums + m.cd[k, j]
            z_sums(k + 1, sums)
            z_gather_forward(k + 1)
            coeff = coefficients(solve_coarse(k + 1), coeff)

    image_on_faces(ITERS - 1)
    for dc, dx in reversed(wide):
        slot = m.fd.at[c_at(-dc), x_at(-dx)]
        remote(slot, slot, m.fss.at[dc, dx], m.frs.at[dc, dx], cx_peer((dc, dx))).wait_recv()
    sums = m.fd[0, 0]
    for i in range(nc):
        for j in range(nx):
            if i or j:
                sums = sums + m.fd[i, j]
    z_sums(0, sums)
    sums = z_sums_total(0)
    _, ratio, alpha = coefficients(sums, coeff)
    z = m.z.at[ITERS - 1]
    t = m.t.at[ITERS - 1]

    def finish(at):
        m.out[0, at, :] = m.x[at, :] + alpha * (z[at, :] + ratio * m.d[at, :])
        m.out[1, at, :] = m.r[at, :] - alpha * (t[at, :] + ratio * m.s[at, :])
    half = ORDER // 2
    outs = []
    for i in range(2):
        loop_rows(i * half, half, finish)
        at = pl.ds(i * half, half)
        for j, into in enumerate((x_out, r_out)):
            outs.append(pltpu.make_async_copy(m.out.at[j, at, :], into.at[0, 0, at, :], m.lsem.at[2 * i + j]))
            outs[-1].start()
    for copy in outs:
        copy.wait()
    for copy in pending:
        copy.wait_send()


class Names:
    def __init__(self, names, refs):
        for name, ref in zip(names, refs, strict=True):
            setattr(self, name, ref)


def scratch(nx, nz, nc, width):
    vmem, dma = pltpu.VMEM, pltpu.SemaphoreType.DMA
    span = nz * MODES
    full, face = (ORDER, width), (FACE_ROWS, width)
    return dict(
        raw=vmem(full, F32), braw=vmem((MODES, ORDER), F32), mraw=vmem((MODES, nx * span), F32), craw=vmem((ORDER, ORDER), F32),
        fbs=pltpu.SMEM((4, nx * nz), jnp.int32), ers=pltpu.SMEM((2, 2, nx * nz), jnp.int32),
        chi=vmem((ORDER, ORDER), BF16), clo=vmem((ORDER, ORDER), BF16), vhi=vmem(full, BF16), vlo=vmem(full, BF16),
        bhl=vmem((2 * MODES, ORDER), BF16), bt=vmem((ORDER, BLOCK), BF16), bpt=vmem((FACE_ROWS, BLOCK), BF16), bph=vmem((4, 2 * MODES, BLOCK), BF16),
        hs=vmem((ITERS, 4, MODES, width), F32), hr=vmem((ITERS, 4, MODES, width), F32), hss=dma((ITERS, 4)), hrs=dma((ITERS, 4)),
        yk=vmem((5, BLOCK, width), BF16), mt=vmem((nx, MODES, span), F32), mhl=vmem((2 * nx * MODES, span), BF16),
        zg=vmem((ITERS, nz, MODES, width), F32), xs=vmem((ITERS, nx, PACK, width), F32), xr=vmem((ITERS, nx, PACK, width), F32),
        yo=vmem((ITERS, MODES, width), F32), yp=vmem((ITERS, 4, MODES, width), F32),
        ts=vmem((ITERS, *face), F32), tp=vmem((ITERS, *face), F32), cd=vmem((ITERS, nc, SUMS, width), F32),
        own=vmem((ITERS, SUMS, width), F32), dz=vmem((ITERS, nz, SUMS, width), F32), fd=vmem((nc, nx, SUMS, width), F32),
        bfs=vmem((4, MODES, BLOCK), F32), bfr=vmem((4, MODES, BLOCK), F32), rp=vmem(face, F32),
        z=vmem((ITERS, *full), F32), t=vmem((ITERS, *full), F32), q=vmem(full, F32), s=vmem(full, F32), r=vmem(full, F32),
        d=vmem(full, F32), x=vmem(full, F32), zp=vmem(face, F32), qp=vmem(face, F32), wp=vmem(face, F32), inner=vmem(face, F32), weight=vmem(face, F32), out=vmem((2, *full), F32),
        lsem=dma((8,)), zss=dma((ITERS, nz + 1)), zrs=dma((ITERS, nz + 1)), xss=dma((ITERS, nx)), xrs=dma((ITERS, nx)),
        yss=dma((ITERS, 4)), yrs=dma((ITERS, 4)), tss=dma((ITERS, 4)), trs=dma((ITERS, 4)), css=dma((ITERS, nc)), crs=dma((ITERS, nc)),
        dzs=dma((ITERS, nz)), dzr=dma((ITERS, nz)), fss=dma((nc, nx)), frs=dma((nc, nx)), mss=dma((nx,)), mrs=dma((nx,)),
        bss=dma((4,)), brs=dma((4,)), rss=dma((4,)), rrs=dma((4,)),
    )


def back_in_place(place_in, x, r, x_out, r_out, held, place, get, put, place_sem):
    pairs = [(p, j) for p in range(NBLOCKS) for j in range(2)]
    sources, intos = (x, r), (x_out, r_out)

    def load(p, j):
        at = pl.ds(p * BLOCK, BLOCK)
        return pltpu.make_async_copy(sources[j].at[0, 0, at, :], held.at[j, at, :], get.at[j, p])

    def store(p, j):
        at = pl.ds(pl.multiple_of(place[p] * BLOCK, BLOCK), BLOCK)
        return pltpu.make_async_copy(held.at[j, pl.ds(p * BLOCK, BLOCK), :], intos[j].at[0, 0, at, :], put.at[j, p])

    get_place = pltpu.make_async_copy(place_in, place, place_sem)
    get_place.start()
    for p, j in pairs:
        load(p, j).start()
    get_place.wait()
    for p, j in pairs:
        load(p, j).wait()
        store(p, j).start()
    for p, j in pairs:
        store(p, j).wait()


def shards(nx, nz, nc, compliance, loads, modes, coarse_inverse, face_block, edge_rows):
    width = loads.shape[-1]
    held = scratch(nx, nz, nc, width)

    def body(*refs):
        kernel(nx, nz, nc, *refs[:9], Names(held, refs[9:]))

    anywhere = pl.BlockSpec(memory_space=pl.ANY)
    small = pl.BlockSpec(memory_space=pltpu.SMEM)
    shapes = [jax.ShapeDtypeStruct(loads.shape, F32)] * 2
    x, r, place = pl.pallas_call(
        body,
        out_shape=shapes + [jax.ShapeDtypeStruct((NBLOCKS,), jnp.int32)],
        in_specs=[anywhere] * 6,
        out_specs=[anywhere, anywhere, small],
        scratch_shapes=list(held.values()),
        compiler_params=pltpu.CompilerParams(collective_id=0, has_side_effects=True, vmem_limit_bytes=56 * 1024 * 1024),
    )(compliance, loads, modes, coarse_inverse, jnp.transpose(face_block, (0, 2, 1)), jnp.transpose(edge_rows, (0, 2, 1)))
    return pl.pallas_call(
        back_in_place,
        out_shape=shapes,
        in_specs=[anywhere] * 3,
        out_specs=[anywhere, anywhere],
        scratch_shapes=[
            pltpu.VMEM((2, ORDER, width), F32), pltpu.SMEM((NBLOCKS,), jnp.int32),
            pltpu.SemaphoreType.DMA((2, NBLOCKS)), pltpu.SemaphoreType.DMA((2, NBLOCKS)), pltpu.SemaphoreType.DMA,
        ],
    )(place, x, r)


def solution(mesh, nz=NZ):
    nc, ns = mesh.shape["cluster"], mesh.shape["sub"]
    cut = P("cluster", "sub", None, None)
    return jax.shard_map(
        functools.partial(shards, ns // nz, nz, nc), mesh=mesh,
        in_specs=(cut, cut, cut, P("cluster", "sub", None), P(), P()),
        out_specs=(cut, cut), check_vma=False,
    )
```

```python
import functools

import jax
import jax.numpy as jnp
from jax import lax
from jax.experimental import pallas as pl
from jax.experimental.pallas import tpu as pltpu
from jax.sharding import PartitionSpec as P

BLOCK = 128
NBLOCKS = 8
ORDER = BLOCK * NBLOCKS
FACE_ROWS = 4 * BLOCK
MODES = 32
SUMS = 2
PACK = MODES + 8
ITERS = 3
NZ = 8
CHUNK = 64
WIDE = 256
F32 = jnp.float32
BF16 = jnp.bfloat16


def split(value):
    high = value.astype(BF16)
    return high, (value - high.astype(F32)).astype(BF16)


def mm(left, right):
    return jnp.dot(left, right, preferred_element_type=F32)


def same(left, right):
    gap = left - right
    return 1 - jnp.minimum(gap * gap, 1)


def fold(value):
    rows, width = value.shape
    return jnp.sum(value.reshape(rows // 8, 8, width), axis=0)


def remote(src, dst, send_sem, recv_sem, device):
    return pltpu.make_async_remote_copy(
        src_ref=src, dst_ref=dst, send_sem=send_sem, recv_sem=recv_sem,
        device_id=device, device_id_type=pl.DeviceIdType.MESH,
    )


def kernel(nx, nz, nc, comp, loads, modes, cinv, fb, er, x_out, r_out, place_out, m):
    ns = nx * nz
    c = lax.axis_index("cluster")
    s = lax.axis_index("sub")
    xm = lax.div(s, nz)
    zm = lax.rem(s, nz)
    width = m.raw.shape[1]

    def z_at(step):
        return lax.rem(zm + (step + nz), nz)

    def x_at(step):
        return lax.rem(xm + (step + nx), nx)

    def c_at(step):
        return lax.rem(c + (step + nc), nc)

    def z_peer(step):
        return (c, xm * nz + z_at(step))

    def x_peer(step):
        return (c, x_at(step) * nz + zm)

    def c_peer(step):
        return (c_at(step), s)

    def cx_peer(step):
        return (c_at(step[0]), x_at(step[1]) * nz + zm)

    beside = (
        (c, lax.rem(s + ns - 1, ns)),
        (c, lax.rem(s + 1, ns)),
        (c_at(-1), s),
        (c_at(1), s),
    )

    get_loads = pltpu.make_async_copy(loads.at[0, 0], m.raw, m.lsem.at[0])
    get_modes = pltpu.make_async_copy(modes.at[0, 0], m.braw, m.lsem.at[1])
    get_cinv = pltpu.make_async_copy(cinv.at[0], m.mraw, m.lsem.at[2])
    get_comp = pltpu.make_async_copy(comp.at[0, 0], m.craw, m.lsem.at[3])
    get_fb = pltpu.make_async_copy(fb.at[c], m.fbs, m.lsem.at[4])
    get_er = pltpu.make_async_copy(er.at[c], m.ers.at[0], m.lsem.at[5])
    get_er_low = pltpu.make_async_copy(er.at[jnp.maximum(c - 1, 0)], m.ers.at[1], m.lsem.at[6])
    for copy in (get_fb, get_er, get_er_low, get_loads, get_modes, get_cinv, get_comp):
        copy.start()

    barrier = pltpu.get_barrier_semaphore()
    wide = sorted(
        ((dc, dx) for dc in range(nc) for dx in range(nx) if dc or dx),
        key=lambda d: -min(d[0], nc - d[0]) - 2 * min(d[1], nx - d[1]),
    )
    greeted = [z_peer(step) for step in range(1, nz)] + [cx_peer(d) for d in wide] + [beside[0], beside[1]]
    for peer in greeted:
        pl.semaphore_signal(barrier, inc=1, device_id=peer, device_id_type=pl.DeviceIdType.MESH)

    for copy in (get_fb, get_er, get_er_low):
        copy.wait()
    faces = [m.fbs[f, s] for f in range(4)]
    rank = jnp.int32(0)
    place = [jnp.int32(0)] * NBLOCKS
    pick = [[] for _ in range(NBLOCKS)]
    for b in range(NBLOCKS):
        hits = [same(face, b) for face in faces]
        free = 1 - (hits[0] + hits[1] + hits[2] + hits[3])
        hits = hits + [free * same(rank, j) for j in range(4)]
        for p in range(NBLOCKS):
            pick[p].append(hits[p].astype(F32))
            place[p] = place[p] + b * hits[p]
        rank = rank + free

    def gathered(p, parts):
        value = pick[p][0] * parts[0]
        for b in range(1, NBLOCKS):
            value = value + pick[p][b] * parts[b]
        return value

    for p in range(NBLOCKS):
        place_out[p] = place[p]

    shared = [
        m.ers[0, 0, jnp.maximum(s - 1, 0)] * jnp.minimum(s, 1),
        m.ers[0, 0, s] * jnp.minimum(ns - 1 - s, 1),
        m.ers[1, 1, s] * jnp.minimum(c, 1),
        m.ers[0, 1, s] * jnp.minimum(nc - 1 - c, 1),
    ]
    row_at = lax.broadcasted_iota(jnp.int32, (BLOCK, width), 0)
    for f in range(4):
        m.weight[pl.ds(f * BLOCK, BLOCK), :] = 0.5 * jnp.clip(shared[f] - row_at, 0, 1).astype(F32)

    def halved(face, value):
        return m.weight[pl.ds(face * BLOCK, BLOCK), :] * value

    def rows(p):
        return pl.ds(p * BLOCK, BLOCK)

    def loop_rows(first, count, body):
        def step(i, carry):
            body(pl.ds(pl.multiple_of(first + i * CHUNK, CHUNK), CHUNK))
            return carry
        lax.fori_loop(0, count // CHUNK, step, 0)

    def to_halves(source):
        def body(at):
            high, low = split(source[at, :])
            m.vhi[at, :] = high
            m.vlo[at, :] = low
        return body

    get_modes.wait()
    high, low = split(m.braw[...])
    m.bhl[0:MODES, :] = high
    m.bhl[MODES:2 * MODES, :] = low
    get_loads.wait()
    loop_rows(0, ORDER, to_halves(m.raw))

    def coarse(first, count):
        ks = pl.ds(first, count)
        both = mm(m.bhl[:, ks], m.vhi[ks, :])
        return both[:MODES] + both[MODES:] + mm(m.bhl[0:MODES, ks], m.vlo[ks, :])

    pending = []

    def send(src, dst, send_sem, recv_sem, device):
        copy = remote(src, dst, send_sem, recv_sem, device)
        copy.start()
        pending.append(copy)

    far_first = sorted(range(1, nz), key=lambda step: -min(step, nz - step))

    early = MODES // 2

    def z_gather_start(k):
        for step in (2, nz - 2, 1, nz - 1):
            mine = m.zg.at[k, zm]
            send(mine, mine, m.zss.at[k, step], m.zrs.at[k, step], z_peer(step))

    def z_wait(k, step, sem, first=0, count=MODES):
        slot = m.zg.at[k, z_at(-step), pl.ds(first, count), :]
        remote(slot, slot, m.zss.at[k, sem], m.zrs.at[k, sem], z_peer(step)).wait_recv()

    def z_gather_forward(k):
        for sign, first, count, sem in ((1, 0, early, 4), (-1, early, MODES - early, nz)):
            z_wait(k, 2 * sign, (2 * sign) % nz)
            slot = m.zg.at[k, z_at(-2 * sign)]
            step = (3 * sign) % nz
            send(slot, slot, m.zss.at[k, step], m.zrs.at[k, step], z_peer(sign))
            slot = m.zg.at[k, z_at(-2 * sign), pl.ds(first, count), :]
            send(slot, slot, m.zss.at[k, sem], m.zrs.at[k, sem], z_peer(2 * sign))

    def z_sums(k, value):
        m.dz[k, zm] = value
        for step in far_first:
            mine = m.dz.at[k, zm]
            send(mine, mine, m.dzs.at[k, step], m.dzr.at[k, step], z_peer(step))

    def z_sums_total(k):
        for step in reversed(far_first):
            slot = m.dz.at[k, z_at(-step)]
            remote(slot, slot, m.dzs.at[k, step], m.dzr.at[k, step], z_peer(step)).wait_recv()
        total = m.dz[k, 0]
        for j in range(1, nz):
            total = total + m.dz[k, j]
        return total

    def z_gather_wait(k):
        for step in (1, -1, 3, -3):
            z_wait(k, step, step % nz)
        z_wait(k, 4, 4, 0, early)
        z_wait(k, 4, nz, early, MODES - early)

    m.zg[0, zm] = coarse(0, ORDER)
    pl.semaphore_wait(barrier, len(greeted))
    z_gather_start(0)

    get_cinv.wait()
    span = nz * MODES
    for step in range(1, nx):
        src = m.mraw.at[:, pl.ds(pl.multiple_of(x_at(step) * span, BLOCK), span)]
        send(src, m.mt.at[xm], m.mss.at[step], m.mrs.at[step], x_peer(step))
    m.mt[xm] = m.mraw[:, pl.ds(pl.multiple_of(xm * span, BLOCK), span)]
    for k in range(ITERS):
        m.xs[k, :, MODES:PACK, :] = jnp.zeros((nx, PACK - MODES, width), F32)
    modes_at = [m.braw[:, rows(b)] for b in range(NBLOCKS)]
    for p in range(NBLOCKS):
        part = gathered(p, modes_at)
        high, low = split(part)
        m.bhl[0:MODES, rows(p)] = high
        m.bhl[MODES:2 * MODES, rows(p)] = low
        if p < 4:
            m.bfs[p] = part
    for f in range(4):
        send(m.bfs.at[f], m.bfr.at[f ^ 1], m.bss.at[f], m.brs.at[f ^ 1], beside[f])

    def in_blocks(i, carry):
        parts = [m.raw[pl.ds(pl.multiple_of(b * BLOCK + i * 8, 8), 8), :] for b in range(NBLOCKS)]
        for p in range(NBLOCKS):
            m.r[pl.ds(pl.multiple_of(p * BLOCK + i * 8, 8), 8), :] = gathered(p, parts)
        return carry

    def columns_in_order(i, carry):
        at = pl.ds(pl.multiple_of(i * 16, 16), 16)
        parts = [m.craw[at, rows(b)] for b in range(NBLOCKS)]
        values = [gathered(q, parts) for q in range(NBLOCKS)]
        for q in range(NBLOCKS):
            m.craw[at, rows(q)] = values[q]
        return carry

    def rows_in_order(i, carry):
        for q in range(NBLOCKS):
            parts = [m.craw[pl.ds(pl.multiple_of(b * BLOCK + i * 16, 16), 16), rows(q)] for b in range(NBLOCKS)]
            for p in range(NBLOCKS):
                at = pl.ds(pl.multiple_of(p * BLOCK + i * 16, 16), 16)
                high, low = split(gathered(p, parts))
                m.chi[at, rows(q)] = high
                m.clo[at, rows(q)] = low
        return carry

    lax.fori_loop(0, BLOCK // 8, in_blocks, 0)
    get_comp.wait()
    lax.fori_loop(0, ORDER // 16, columns_in_order, 0)
    z_gather_forward(0)
    for f in range(4):
        remote(m.r.at[rows(f), :], m.rp.at[rows(f ^ 1), :], m.rss.at[f], m.rrs.at[f ^ 1], beside[f]).start()

    def transposed(high, low):
        stacked = jnp.concatenate([high.astype(F32), low.astype(F32), high.astype(F32), jnp.zeros((MODES, BLOCK), F32)], axis=0)
        return stacked.T.astype(BF16)

    for p in range(NBLOCKS):
        m.bt[rows(p), :] = transposed(m.bhl[0:MODES, rows(p)], m.bhl[MODES:2 * MODES, rows(p)])
    m.yk[:, 3 * MODES:, :] = jnp.zeros((5, MODES, width), BF16)
    lax.fori_loop(0, BLOCK // 16, rows_in_order, 0)

    for step in range(1, nx):
        slot = m.mt.at[x_at(-step)]
        remote(slot, slot, m.mss.at[step], m.mrs.at[step], x_peer(step)).wait_recv()
    high, low = split(m.mt[...].reshape(nx * MODES, span))
    m.mhl[0:nx * MODES, :] = high
    m.mhl[nx * MODES:, :] = low
    for f in range(4):
        slot = m.bfr.at[f]
        remote(slot, slot, m.bss.at[f], m.brs.at[f], beside[f]).wait_recv()
        high, low = split(m.bfr[f])
        m.bpt[rows(f), :] = transposed(high, low)
        m.bph[f, 0:MODES, :] = high
        m.bph[f, MODES:2 * MODES, :] = low

    def stack_y(i, value):
        high, low = split(value)
        m.yk[i, 0:MODES, :] = high
        m.yk[i, MODES:2 * MODES, :] = high
        m.yk[i, 2 * MODES:3 * MODES, :] = low

    def send_faces(k):
        for f in (2, 3, 0, 1):
            send(m.ts.at[k, rows(f), :], m.tp.at[k, rows(f ^ 1), :], m.tss.at[k, f], m.trs.at[k, f ^ 1], beside[f])

    def image_on_faces(k):
        for f in range(4):
            slot = m.tp.at[k, rows(f), :]
            remote(slot, slot, m.tss.at[k, f], m.trs.at[k, f], beside[f]).wait_recv()
        for f in range(4):
            own = m.ts[k, rows(f), :]
            theirs = m.tp[k, rows(f), :]
            m.t[k, rows(f), :] = own + halved(f, theirs)
            if k + 1 < ITERS:
                m.wp[rows(f), :] = theirs + halved(f, own)

    def solve_coarse(k):
        z_gather_wait(k)
        high, low = split(m.zg[k].reshape(nz * MODES, width))
        both = mm(m.mhl[...], high)
        half = nx * MODES
        part = both[:half] + both[half:] + mm(m.mhl[0:half, :], low)
        m.xs[k, :, 0:MODES, :] = part.reshape(nx, MODES, width)
        if k > 0:
            sums = z_sums_total(k)
            for j in range(nx):
                m.xs[k, j, MODES:MODES + SUMS, :] = sums
        for step in range(1, nx):
            send(m.xs.at[k, x_at(step)], m.xr.at[k, xm], m.xss.at[k, step], m.xrs.at[k, step], x_peer(step))
        m.xr[k, xm] = m.xs[k, xm]
        for step in range(1, nx):
            slot = m.xr.at[k, x_at(-step)]
            remote(slot, slot, m.xss.at[k, step], m.xrs.at[k, step], x_peer(step)).wait_recv()
        total = m.xr[k, 0]
        for j in range(1, nx):
            total = total + m.xr[k, j]
        m.yo[k] = total[:MODES]
        for f in range(4):
            send(m.yo.at[k], m.yp.at[k, f ^ 1], m.yss.at[k, f], m.yrs.at[k, f ^ 1], beside[f])
        stack_y(4, total[:MODES])
        return total[MODES:MODES + SUMS]

    def wait_y(k, f):
        slot = m.yp.at[k, f]
        remote(slot, slot, m.yss.at[k, f], m.yrs.at[k, f], beside[f]).wait_recv()

    def product(at, ks):
        return mm(m.chi[at, ks], m.vhi[ks, :]) + mm(m.chi[at, ks], m.vlo[ks, :]) + mm(m.clo[at, ks], m.vhi[ks, :])

    def keep_halves(at, value):
        high, low = split(value)
        m.vhi[at, :] = high
        m.vlo[at, :] = low

    near, inside = pl.ds(0, FACE_ROWS), pl.ds(FACE_ROWS, ORDER - FACE_ROWS)
    near_parts = [pl.ds(i, WIDE) for i in range(0, FACE_ROWS, WIDE)]
    inside_parts = [pl.ds(i, WIDE) for i in range(FACE_ROWS, ORDER, WIDE)]

    def coefficients(sums, old):
        rz, curve = sums[0:1], sums[1:2]
        if old is None:
            return rz, None, rz / curve
        ratio = rz / old[0]
        return rz, ratio, rz / (curve - ratio * rz / old[2])

    solve_coarse(0)
    coeff = None
    for k in range(ITERS):
        z = m.z.at[k]
        t = m.t.at[k]
        if k > 0:
            w = m.t.at[k - 1]
            z_old = m.z.at[k - 1]
            _, ratio, alpha = coeff
        def new_z(at):
            value = mm(m.bt[at, :], m.yk[4])
            if k == 0:
                value = m.r[at, :] + value
            else:
                value = w[at, :] + value
                if ratio is not None:
                    value = value + ratio * m.q[at, :]
                m.q[at, :] = value
                value = z_old[at, :] - alpha * value
            z[at, :] = value
            return value
        for at in inside_parts:
            keep_halves(at, new_z(at))
        for at in near_parts + inside_parts:
            t[at, :] = product(at, inside)
        if k > 0:
            image_on_faces(k - 1)
        for at in near_parts:
            new_z(at)
        def update(i, total, z=z):
            at = pl.ds(pl.multiple_of(i * CHUNK, CHUNK), CHUNK)
            r = m.r[at, :]
            if k > 0:
                s_new, d_new = w[at, :], z_old[at, :]
                if ratio is not None:
                    s_new = s_new + ratio * m.s[at, :]
                    d_new = d_new + ratio * m.d[at, :]
                m.s[at, :] = s_new
                m.d[at, :] = d_new
                m.x[at, :] = alpha * d_new if k == 1 else m.x[at, :] + alpha * d_new
                r = r - alpha * s_new
                m.r[at, :] = r
            return total + fold(r * z[at, :])
        zero = jnp.zeros((8, width), F32)
        first = lax.fori_loop(0, ORDER // CHUNK, update, zero)
        m.own[k, 0:1, :] = jnp.sum(first, axis=0, keepdims=True)
        for f in (2, 3, 0, 1):
            wait_y(k, f)
            if k == 0:
                slot = m.rp.at[rows(f), :]
                copy = remote(slot, slot, m.rss.at[f], m.rrs.at[f], beside[f])
                copy.wait_recv()
                copy.wait_send()
        for f in range(4):
            stack_y(f, m.yp[k, f])
        for f in range(4):
            value = mm(m.bpt[rows(f), :], m.yk[f])
            if k == 0:
                value = m.rp[rows(f), :] + value
            else:
                value = m.wp[rows(f), :] + value
                if ratio is not None:
                    value = value + ratio * m.qp[rows(f), :]
                m.qp[rows(f), :] = value
                value = m.zp[rows(f), :] - alpha * value
            m.zp[rows(f), :] = value
            inner = z[rows(f), :] + halved(f, value)
            m.inner[rows(f), :] = inner
            keep_halves(rows(f), inner)
        for f in range(4):
            m.ts[k, rows(f), :] = t[rows(f), :] + product(rows(f), near)
        if k + 1 < ITERS:
            for f in range(4):
                high, low = split(halved(f, m.ts[k, rows(f), :]))
                both = mm(m.bph[f], high)
                m.hs[k, f] = both[:MODES] + both[MODES:] + mm(m.bph[f, 0:MODES, :], low)
                send(m.hs.at[k, f], m.hr.at[k, f ^ 1], m.hss.at[k, f], m.hrs.at[k, f ^ 1], beside[f])
            send_faces(k)
        else:
            send_faces(k)
        def dots(i, total, z=z, t=t, k=k):
            at = pl.ds(pl.multiple_of(i * CHUNK, CHUNK), CHUNK)
            low_at = pl.ds(pl.multiple_of(FACE_ROWS + i * CHUNK, CHUNK), CHUNK)
            return total + fold(m.inner[at, :] * (m.ts[k, at, :] + t[at, :])) + fold(z[low_at, :] * t[low_at, :])
        second = lax.fori_loop(0, FACE_ROWS // CHUNK, dots, zero)
        m.own[k, 1:2, :] = jnp.sum(second, axis=0, keepdims=True)
        if k + 1 < ITERS:
            m.cd[k, c] = m.own[k]
            for step in range(1, nc):
                mine = m.cd.at[k, c]
                send(mine, mine, m.css.at[k, step], m.crs.at[k, step], c_peer(step))
        else:
            m.fd[c, xm] = m.own[k]
            for dc, dx in wide:
                mine = m.fd.at[c, xm]
                send(mine, mine, m.fss.at[dc, dx], m.frs.at[dc, dx], cx_peer((dc, dx)))
        for at in inside_parts:
            value = t[at, :] + product(at, near)
            t[at, :] = value
            if k + 1 < ITERS:
                keep_halves(at, value)

        if k + 1 < ITERS:
            for at in near_parts:
                keep_halves(at, m.ts[k, at, :])
            part = coarse(0, ORDER)
            for f in range(4):
                slot = m.hr.at[k, f]
                remote(slot, slot, m.hss.at[k, f], m.hrs.at[k, f], beside[f]).wait_recv()
                part = part + m.hr[k, f]
            m.zg[k + 1, zm] = part
            z_gather_start(k + 1)
            for step in range(1, nc):
                slot = m.cd.at[k, c_at(-step)]
                remote(slot, slot, m.css.at[k, step], m.crs.at[k, step], c_peer(step)).wait_recv()
            sums = m.cd[k, 0]
            for j in range(1, nc):
                sums = sums + m.cd[k, j]
            z_sums(k + 1, sums)
            z_gather_forward(k + 1)
            coeff = coefficients(solve_coarse(k + 1), coeff)

    image_on_faces(ITERS - 1)
    for dc, dx in reversed(wide):
        slot = m.fd.at[c_at(-dc), x_at(-dx)]
        remote(slot, slot, m.fss.at[dc, dx], m.frs.at[dc, dx], cx_peer((dc, dx))).wait_recv()
    sums = m.fd[0, 0]
    for i in range(nc):
        for j in range(nx):
            if i or j:
                sums = sums + m.fd[i, j]
    z_sums(0, sums)
    sums = z_sums_total(0)
    _, ratio, alpha = coefficients(sums, coeff)
    z = m.z.at[ITERS - 1]
    t = m.t.at[ITERS - 1]

    def finish(at):
        m.out[0, at, :] = m.x[at, :] + alpha * (z[at, :] + ratio * m.d[at, :])
        m.out[1, at, :] = m.r[at, :] - alpha * (t[at, :] + ratio * m.s[at, :])
    half = ORDER // 2
    outs = []
    for i in range(2):
        loop_rows(i * half, half, finish)
        at = pl.ds(i * half, half)
        for j, into in enumerate((x_out, r_out)):
            outs.append(pltpu.make_async_copy(m.out.at[j, at, :], into.at[0, 0, at, :], m.lsem.at[2 * i + j]))
            outs[-1].start()
    for copy in outs:
        copy.wait()
    for copy in pending:
        copy.wait_send()


class Names:
    def __init__(self, names, refs):
        for name, ref in zip(names, refs, strict=True):
            setattr(self, name, ref)


def scratch(nx, nz, nc, width):
    vmem, dma = pltpu.VMEM, pltpu.SemaphoreType.DMA
    span = nz * MODES
    full, face = (ORDER, width), (FACE_ROWS, width)
    return dict(
        raw=vmem(full, F32), braw=vmem((MODES, ORDER), F32), mraw=vmem((MODES, nx * span), F32), craw=vmem((ORDER, ORDER), F32),
        fbs=pltpu.SMEM((4, nx * nz), jnp.int32), ers=pltpu.SMEM((2, 2, nx * nz), jnp.int32),
        chi=vmem((ORDER, ORDER), BF16), clo=vmem((ORDER, ORDER), BF16), vhi=vmem(full, BF16), vlo=vmem(full, BF16),
        bhl=vmem((2 * MODES, ORDER), BF16), bt=vmem((ORDER, BLOCK), BF16), bpt=vmem((FACE_ROWS, BLOCK), BF16), bph=vmem((4, 2 * MODES, BLOCK), BF16),
        hs=vmem((ITERS, 4, MODES, width), F32), hr=vmem((ITERS, 4, MODES, width), F32), hss=dma((ITERS, 4)), hrs=dma((ITERS, 4)),
        yk=vmem((5, BLOCK, width), BF16), mt=vmem((nx, MODES, span), F32), mhl=vmem((2 * nx * MODES, span), BF16),
        zg=vmem((ITERS, nz, MODES, width), F32), xs=vmem((ITERS, nx, PACK, width), F32), xr=vmem((ITERS, nx, PACK, width), F32),
        yo=vmem((ITERS, MODES, width), F32), yp=vmem((ITERS, 4, MODES, width), F32),
        ts=vmem((ITERS, *face), F32), tp=vmem((ITERS, *face), F32), cd=vmem((ITERS, nc, SUMS, width), F32),
        own=vmem((ITERS, SUMS, width), F32), dz=vmem((ITERS, nz, SUMS, width), F32), fd=vmem((nc, nx, SUMS, width), F32),
        bfs=vmem((4, MODES, BLOCK), F32), bfr=vmem((4, MODES, BLOCK), F32), rp=vmem(face, F32),
        z=vmem((ITERS, *full), F32), t=vmem((ITERS, *full), F32), q=vmem(full, F32), s=vmem(full, F32), r=vmem(full, F32),
        d=vmem(full, F32), x=vmem(full, F32), zp=vmem(face, F32), qp=vmem(face, F32), wp=vmem(face, F32), inner=vmem(face, F32), weight=vmem(face, F32), out=vmem((2, *full), F32),
        lsem=dma((8,)), zss=dma((ITERS, nz + 1)), zrs=dma((ITERS, nz + 1)), xss=dma((ITERS, nx)), xrs=dma((ITERS, nx)),
        yss=dma((ITERS, 4)), yrs=dma((ITERS, 4)), tss=dma((ITERS, 4)), trs=dma((ITERS, 4)), css=dma((ITERS, nc)), crs=dma((ITERS, nc)),
        dzs=dma((ITERS, nz)), dzr=dma((ITERS, nz)), fss=dma((nc, nx)), frs=dma((nc, nx)), mss=dma((nx,)), mrs=dma((nx,)),
        bss=dma((4,)), brs=dma((4,)), rss=dma((4,)), rrs=dma((4,)),
    )


def back_in_place(place_in, x, r, x_out, r_out, held, place, get, put, place_sem):
    pairs = [(p, j) for p in range(NBLOCKS) for j in range(2)]
    sources, intos = (x, r), (x_out, r_out)

    def load(p, j):
        at = pl.ds(p * BLOCK, BLOCK)
        return pltpu.make_async_copy(sources[j].at[0, 0, at, :], held.at[j, at, :], get.at[j, p])

    def store(p, j):
        at = pl.ds(pl.multiple_of(place[p] * BLOCK, BLOCK), BLOCK)
        return pltpu.make_async_copy(held.at[j, pl.ds(p * BLOCK, BLOCK), :], intos[j].at[0, 0, at, :], put.at[j, p])

    get_place = pltpu.make_async_copy(place_in, place, place_sem)
    get_place.start()
    for p, j in pairs:
        load(p, j).start()
    get_place.wait()
    for p, j in pairs:
        load(p, j).wait()
        store(p, j).start()
    for p, j in pairs:
        store(p, j).wait()


def shards(nx, nz, nc, compliance, loads, modes, coarse_inverse, face_block, edge_rows):
    width = loads.shape[-1]
    held = scratch(nx, nz, nc, width)

    def body(*refs):
        kernel(nx, nz, nc, *refs[:9], Names(held, refs[9:]))

    anywhere = pl.BlockSpec(memory_space=pl.ANY)
    small = pl.BlockSpec(memory_space=pltpu.SMEM)
    shapes = [jax.ShapeDtypeStruct(loads.shape, F32)] * 2
    x, r, place = pl.pallas_call(
        body,
        out_shape=shapes + [jax.ShapeDtypeStruct((NBLOCKS,), jnp.int32)],
        in_specs=[anywhere] * 6,
        out_specs=[anywhere, anywhere, small],
        scratch_shapes=list(held.values()),
        compiler_params=pltpu.CompilerParams(collective_id=0, has_side_effects=True, vmem_limit_bytes=56 * 1024 * 1024),
    )(compliance, loads, modes, coarse_inverse, jnp.transpose(face_block, (0, 2, 1)), jnp.transpose(edge_rows, (0, 2, 1)))
    return pl.pallas_call(
        back_in_place,
        out_shape=shapes,
        in_specs=[anywhere] * 3,
        out_specs=[anywhere, anywhere],
        scratch_shapes=[
            pltpu.VMEM((2, ORDER, width), F32), pltpu.SMEM((NBLOCKS,), jnp.int32),
            pltpu.SemaphoreType.DMA((2, NBLOCKS)), pltpu.SemaphoreType.DMA((2, NBLOCKS)), pltpu.SemaphoreType.DMA,
        ],
    )(place, x, r)


def solution(mesh, nz=NZ):
    nc, ns = mesh.shape["cluster"], mesh.shape["sub"]
    cut = P("cluster", "sub", None, None)
    return jax.shard_map(
        functools.partial(shards, ns // nz, nz, nc), mesh=mesh,
        in_specs=(cut, cut, cut, P("cluster", "sub", None), P(), P()),
        out_specs=(cut, cut), check_vma=False,
    )
```

```python
import functools

import jax
import jax.numpy as jnp
from jax import lax
from jax.experimental import pallas as pl
from jax.experimental.pallas import tpu as pltpu
from jax.sharding import PartitionSpec as P

BLOCK = 128
NBLOCKS = 8
ORDER = BLOCK * NBLOCKS
FACE_ROWS = 4 * BLOCK
MODES = 32
SUMS = 2
PACK = MODES + 8
ITERS = 3
NZ = 8
CHUNK = 64
WIDE = 256
F32 = jnp.float32
BF16 = jnp.bfloat16


def split(value):
    high = value.astype(BF16)
    return high, (value - high.astype(F32)).astype(BF16)


def mm(left, right):
    return jnp.dot(left, right, preferred_element_type=F32)


def same(left, right):
    gap = left - right
    return 1 - jnp.minimum(gap * gap, 1)


def fold(value):
    rows, width = value.shape
    return jnp.sum(value.reshape(rows // 8, 8, width), axis=0)


def remote(src, dst, send_sem, recv_sem, device):
    return pltpu.make_async_remote_copy(
        src_ref=src, dst_ref=dst, send_sem=send_sem, recv_sem=recv_sem,
        device_id=device, device_id_type=pl.DeviceIdType.MESH,
    )


def kernel(nx, nz, nc, comp, loads, modes, cinv, fb, er, x_out, r_out, place_out, m):
    ns = nx * nz
    c = lax.axis_index("cluster")
    s = lax.axis_index("sub")
    xm = lax.div(s, nz)
    zm = lax.rem(s, nz)
    width = m.raw.shape[1]

    def z_at(step):
        return lax.rem(zm + (step + nz), nz)

    def x_at(step):
        return lax.rem(xm + (step + nx), nx)

    def c_at(step):
        return lax.rem(c + (step + nc), nc)

    def z_peer(step):
        return (c, xm * nz + z_at(step))

    def x_peer(step):
        return (c, x_at(step) * nz + zm)

    def c_peer(step):
        return (c_at(step), s)

    def cx_peer(step):
        return (c_at(step[0]), x_at(step[1]) * nz + zm)

    beside = (
        (c, lax.rem(s + ns - 1, ns)),
        (c, lax.rem(s + 1, ns)),
        (c_at(-1), s),
        (c_at(1), s),
    )

    get_loads = pltpu.make_async_copy(loads.at[0, 0], m.raw, m.lsem.at[0])
    get_modes = pltpu.make_async_copy(modes.at[0, 0], m.braw, m.lsem.at[1])
    get_cinv = pltpu.make_async_copy(cinv.at[0], m.mraw, m.lsem.at[2])
    get_comp = pltpu.make_async_copy(comp.at[0, 0], m.craw, m.lsem.at[3])
    get_fb = pltpu.make_async_copy(fb.at[c], m.fbs, m.lsem.at[4])
    get_er = pltpu.make_async_copy(er.at[c], m.ers.at[0], m.lsem.at[5])
    get_er_low = pltpu.make_async_copy(er.at[jnp.maximum(c - 1, 0)], m.ers.at[1], m.lsem.at[6])
    for copy in (get_fb, get_er, get_er_low, get_loads, get_modes, get_cinv, get_comp):
        copy.start()

    barrier = pltpu.get_barrier_semaphore()
    wide = sorted(
        ((dc, dx) for dc in range(nc) for dx in range(nx) if dc or dx),
        key=lambda d: -min(d[0], nc - d[0]) - 2 * min(d[1], nx - d[1]),
    )
    greeted = [z_peer(step) for step in range(1, nz)] + [cx_peer(d) for d in wide] + [beside[0], beside[1]]
    for peer in greeted:
        pl.semaphore_signal(barrier, inc=1, device_id=peer, device_id_type=pl.DeviceIdType.MESH)

    for copy in (get_fb, get_er, get_er_low):
        copy.wait()
    faces = [m.fbs[f, s] for f in range(4)]
    rank = jnp.int32(0)
    place = [jnp.int32(0)] * NBLOCKS
    pick = [[] for _ in range(NBLOCKS)]
    for b in range(NBLOCKS):
        hits = [same(face, b) for face in faces]
        free = 1 - (hits[0] + hits[1] + hits[2] + hits[3])
        hits = hits + [free * same(rank, j) for j in range(4)]
        for p in range(NBLOCKS):
            pick[p].append(hits[p].astype(F32))
            place[p] = place[p] + b * hits[p]
        rank = rank + free

    def gathered(p, parts):
        value = pick[p][0] * parts[0]
        for b in range(1, NBLOCKS):
            value = value + pick[p][b] * parts[b]
        return value

    for p in range(NBLOCKS):
        place_out[p] = place[p]

    shared = [
        m.ers[0, 0, jnp.maximum(s - 1, 0)] * jnp.minimum(s, 1),
        m.ers[0, 0, s] * jnp.minimum(ns - 1 - s, 1),
        m.ers[1, 1, s] * jnp.minimum(c, 1),
        m.ers[0, 1, s] * jnp.minimum(nc - 1 - c, 1),
    ]
    row_at = lax.broadcasted_iota(jnp.int32, (BLOCK, width), 0)
    for f in range(4):
        m.weight[pl.ds(f * BLOCK, BLOCK), :] = 0.5 * jnp.clip(shared[f] - row_at, 0, 1).astype(F32)

    def halved(face, value):
        return m.weight[pl.ds(face * BLOCK, BLOCK), :] * value

    def rows(p):
        return pl.ds(p * BLOCK, BLOCK)

    def loop_rows(first, count, body):
        def step(i, carry):
            body(pl.ds(pl.multiple_of(first + i * CHUNK, CHUNK), CHUNK))
            return carry
        lax.fori_loop(0, count // CHUNK, step, 0)

    def to_halves(source):
        def body(at):
            high, low = split(source[at, :])
            m.vhi[at, :] = high
            m.vlo[at, :] = low
        return body

    get_modes.wait()
    high, low = split(m.braw[...])
    m.bhl[0:MODES, :] = high
    m.bhl[MODES:2 * MODES, :] = low
    get_loads.wait()
    loop_rows(0, ORDER, to_halves(m.raw))

    def coarse(first, count):
        ks = pl.ds(first, count)
        both = mm(m.bhl[:, ks], m.vhi[ks, :])
        return both[:MODES] + both[MODES:] + mm(m.bhl[0:MODES, ks], m.vlo[ks, :])

    pending = []

    def send(src, dst, send_sem, recv_sem, device):
        copy = remote(src, dst, send_sem, recv_sem, device)
        copy.start()
        pending.append(copy)

    far_first = sorted(range(1, nz), key=lambda step: -min(step, nz - step))

    early = MODES // 2

    def z_gather_start(k):
        for step in (2, nz - 2, 1, nz - 1):
            mine = m.zg.at[k, zm]
            send(mine, mine, m.zss.at[k, step], m.zrs.at[k, step], z_peer(step))

    def z_wait(k, step, sem, first=0, count=MODES):
        slot = m.zg.at[k, z_at(-step), pl.ds(first, count), :]
        remote(slot, slot, m.zss.at[k, sem], m.zrs.at[k, sem], z_peer(step)).wait_recv()

    def z_gather_forward(k):
        for sign, first, count, sem in ((1, 0, early, 4), (-1, early, MODES - early, nz)):
            z_wait(k, 2 * sign, (2 * sign) % nz)
            slot = m.zg.at[k, z_at(-2 * sign)]
            step = (3 * sign) % nz
            send(slot, slot, m.zss.at[k, step], m.zrs.at[k, step], z_peer(sign))
            slot = m.zg.at[k, z_at(-2 * sign), pl.ds(first, count), :]
            send(slot, slot, m.zss.at[k, sem], m.zrs.at[k, sem], z_peer(2 * sign))

    def z_sums(k, value):
        m.dz[k, zm] = value
        for step in far_first:
            mine = m.dz.at[k, zm]
            send(mine, mine, m.dzs.at[k, step], m.dzr.at[k, step], z_peer(step))

    def z_sums_total(k):
        for step in reversed(far_first):
            slot = m.dz.at[k, z_at(-step)]
            remote(slot, slot, m.dzs.at[k, step], m.dzr.at[k, step], z_peer(step)).wait_recv()
        total = m.dz[k, 0]
        for j in range(1, nz):
            total = total + m.dz[k, j]
        return total

    def z_gather_wait(k):
        for step in (1, -1, 3, -3):
            z_wait(k, step, step % nz)
        z_wait(k, 4, 4, 0, early)
        z_wait(k, 4, nz, early, MODES - early)

    m.zg[0, zm] = coarse(0, ORDER)
    pl.semaphore_wait(barrier, len(greeted))
    z_gather_start(0)

    get_cinv.wait()
    span = nz * MODES
    for step in range(1, nx):
        src = m.mraw.at[:, pl.ds(pl.multiple_of(x_at(step) * span, BLOCK), span)]
        send(src, m.mt.at[xm], m.mss.at[step], m.mrs.at[step], x_peer(step))
    m.mt[xm] = m.mraw[:, pl.ds(pl.multiple_of(xm * span, BLOCK), span)]
    for k in range(ITERS):
        m.xs[k, :, MODES:PACK, :] = jnp.zeros((nx, PACK - MODES, width), F32)
    modes_at = [m.braw[:, rows(b)] for b in range(NBLOCKS)]
    for p in range(NBLOCKS):
        part = gathered(p, modes_at)
        high, low = split(part)
        m.bhl[0:MODES, rows(p)] = high
        m.bhl[MODES:2 * MODES, rows(p)] = low
        if p < 4:
            m.bfs[p] = part
    for f in range(4):
        send(m.bfs.at[f], m.bfr.at[f ^ 1], m.bss.at[f], m.brs.at[f ^ 1], beside[f])

    def in_blocks(i, carry):
        parts = [m.raw[pl.ds(pl.multiple_of(b * BLOCK + i * 8, 8), 8), :] for b in range(NBLOCKS)]
        for p in range(NBLOCKS):
            m.r[pl.ds(pl.multiple_of(p * BLOCK + i * 8, 8), 8), :] = gathered(p, parts)
        return carry

    def columns_in_order(i, carry):
        at = pl.ds(pl.multiple_of(i * 16, 16), 16)
        parts = [m.craw[at, rows(b)] for b in range(NBLOCKS)]
        values = [gathered(q, parts) for q in range(NBLOCKS)]
        for q in range(NBLOCKS):
            m.craw[at, rows(q)] = values[q]
        return carry

    def rows_in_order(i, carry):
        for q in range(NBLOCKS):
            parts = [m.craw[pl.ds(pl.multiple_of(b * BLOCK + i * 16, 16), 16), rows(q)] for b in range(NBLOCKS)]
            for p in range(NBLOCKS):
                at = pl.ds(pl.multiple_of(p * BLOCK + i * 16, 16), 16)
                high, low = split(gathered(p, parts))
                m.chi[at, rows(q)] = high
                m.clo[at, rows(q)] = low
        return carry

    lax.fori_loop(0, BLOCK // 8, in_blocks, 0)
    get_comp.wait()
    lax.fori_loop(0, ORDER // 16, columns_in_order, 0)
    z_gather_forward(0)
    for f in range(4):
        remote(m.r.at[rows(f), :], m.rp.at[rows(f ^ 1), :], m.rss.at[f], m.rrs.at[f ^ 1], beside[f]).start()

    def transposed(high, low):
        stacked = jnp.concatenate([high.astype(F32), low.astype(F32), high.astype(F32), jnp.zeros((MODES, BLOCK), F32)], axis=0)
        return stacked.T.astype(BF16)

    for p in range(NBLOCKS):
        m.bt[rows(p), :] = transposed(m.bhl[0:MODES, rows(p)], m.bhl[MODES:2 * MODES, rows(p)])
    m.yk[:, 3 * MODES:, :] = jnp.zeros((5, MODES, width), BF16)
    lax.fori_loop(0, BLOCK // 16, rows_in_order, 0)

    for step in range(1, nx):
        slot = m.mt.at[x_at(-step)]
        remote(slot, slot, m.mss.at[step], m.mrs.at[step], x_peer(step)).wait_recv()
    high, low = split(m.mt[...].reshape(nx * MODES, span))
    m.mhl[0:nx * MODES, :] = high
    m.mhl[nx * MODES:, :] = low
    for f in range(4):
        slot = m.bfr.at[f]
        remote(slot, slot, m.bss.at[f], m.brs.at[f], beside[f]).wait_recv()
        high, low = split(m.bfr[f])
        m.bpt[rows(f), :] = transposed(high, low)
        m.bph[f, 0:MODES, :] = high
        m.bph[f, MODES:2 * MODES, :] = low

    def stack_y(i, value):
        high, low = split(value)
        m.yk[i, 0:MODES, :] = high
        m.yk[i, MODES:2 * MODES, :] = high
        m.yk[i, 2 * MODES:3 * MODES, :] = low

    def send_faces(k):
        for f in (2, 3, 0, 1):
            send(m.ts.at[k, rows(f), :], m.tp.at[k, rows(f ^ 1), :], m.tss.at[k, f], m.trs.at[k, f ^ 1], beside[f])

    def image_on_faces(k):
        for f in range(4):
            slot = m.tp.at[k, rows(f), :]
            remote(slot, slot, m.tss.at[k, f], m.trs.at[k, f], beside[f]).wait_recv()
        for f in range(4):
            own = m.ts[k, rows(f), :]
            theirs = m.tp[k, rows(f), :]
            m.t[k, rows(f), :] = own + halved(f, theirs)
            if k + 1 < ITERS:
                m.wp[rows(f), :] = theirs + halved(f, own)

    def solve_coarse(k):
        z_gather_wait(k)
        high, low = split(m.zg[k].reshape(nz * MODES, width))
        both = mm(m.mhl[...], high)
        half = nx * MODES
        part = both[:half] + both[half:] + mm(m.mhl[0:half, :], low)
        m.xs[k, :, 0:MODES, :] = part.reshape(nx, MODES, width)
        if k > 0:
            sums = z_sums_total(k)
            for j in range(nx):
                m.xs[k, j, MODES:MODES + SUMS, :] = sums
        for step in range(1, nx):
            send(m.xs.at[k, x_at(step)], m.xr.at[k, xm], m.xss.at[k, step], m.xrs.at[k, step], x_peer(step))
        m.xr[k, xm] = m.xs[k, xm]
        for step in range(1, nx):
            slot = m.xr.at[k, x_at(-step)]
            remote(slot, slot, m.xss.at[k, step], m.xrs.at[k, step], x_peer(step)).wait_recv()
        total = m.xr[k, 0]
        for j in range(1, nx):
            total = total + m.xr[k, j]
        m.yo[k] = total[:MODES]
        for f in range(4):
            send(m.yo.at[k], m.yp.at[k, f ^ 1], m.yss.at[k, f], m.yrs.at[k, f ^ 1], beside[f])
        stack_y(4, total[:MODES])
        return total[MODES:MODES + SUMS]

    def wait_y(k, f):
        slot = m.yp.at[k, f]
        remote(slot, slot, m.yss.at[k, f], m.yrs.at[k, f], beside[f]).wait_recv()

    def product(at, ks):
        return mm(m.chi[at, ks], m.vhi[ks, :]) + mm(m.chi[at, ks], m.vlo[ks, :]) + mm(m.clo[at, ks], m.vhi[ks, :])

    def keep_halves(at, value):
        high, low = split(value)
        m.vhi[at, :] = high
        m.vlo[at, :] = low

    near, inside = pl.ds(0, FACE_ROWS), pl.ds(FACE_ROWS, ORDER - FACE_ROWS)
    near_parts = [pl.ds(i, WIDE) for i in range(0, FACE_ROWS, WIDE)]
    inside_parts = [pl.ds(i, WIDE) for i in range(FACE_ROWS, ORDER, WIDE)]

    def coefficients(sums, old):
        rz, curve = sums[0:1], sums[1:2]
        if old is None:
            return rz, None, rz / curve
        ratio = rz / old[0]
        return rz, ratio, rz / (curve - ratio * rz / old[2])

    solve_coarse(0)
    coeff = None
    for k in range(ITERS):
        z = m.z.at[k]
        t = m.t.at[k]
        if k > 0:
            w = m.t.at[k - 1]
            z_old = m.z.at[k - 1]
            _, ratio, alpha = coeff
        def new_z(at):
            value = mm(m.bt[at, :], m.yk[4])
            if k == 0:
                value = m.r[at, :] + value
            else:
                value = w[at, :] + value
                if ratio is not None:
                    value = value + ratio * m.q[at, :]
                m.q[at, :] = value
                value = z_old[at, :] - alpha * value
            z[at, :] = value
            return value
        for at in inside_parts:
            keep_halves(at, new_z(at))
        for at in near_parts + inside_parts:
            t[at, :] = product(at, inside)
        if k > 0:
            image_on_faces(k - 1)
        for at in near_parts:
            new_z(at)
        def update(i, total, z=z):
            at = pl.ds(pl.multiple_of(i * CHUNK, CHUNK), CHUNK)
            r = m.r[at, :]
            if k > 0:
                s_new, d_new = w[at, :], z_old[at, :]
                if ratio is not None:
                    s_new = s_new + ratio * m.s[at, :]
                    d_new = d_new + ratio * m.d[at, :]
                m.s[at, :] = s_new
                m.d[at, :] = d_new
                m.x[at, :] = alpha * d_new if k == 1 else m.x[at, :] + alpha * d_new
                r = r - alpha * s_new
                m.r[at, :] = r
            return total + fold(r * z[at, :])
        zero = jnp.zeros((8, width), F32)
        first = lax.fori_loop(0, ORDER // CHUNK, update, zero)
        m.own[k, 0:1, :] = jnp.sum(first, axis=0, keepdims=True)
        for f in (2, 3, 0, 1):
            wait_y(k, f)
            if k == 0:
                slot = m.rp.at[rows(f), :]
                copy = remote(slot, slot, m.rss.at[f], m.rrs.at[f], beside[f])
                copy.wait_recv()
                copy.wait_send()
        for f in range(4):
            stack_y(f, m.yp[k, f])
        for f in range(4):
            value = mm(m.bpt[rows(f), :], m.yk[f])
            if k == 0:
                value = m.rp[rows(f), :] + value
            else:
                value = m.wp[rows(f), :] + value
                if ratio is not None:
                    value = value + ratio * m.qp[rows(f), :]
                m.qp[rows(f), :] = value
                value = m.zp[rows(f), :] - alpha * value
            m.zp[rows(f), :] = value
            inner = z[rows(f), :] + halved(f, value)
            m.inner[rows(f), :] = inner
            keep_halves(rows(f), inner)
        for f in range(4):
            value = t[rows(f), :] + product(rows(f), near)
            m.ts[k, rows(f), :] = value
            if k + 1 < ITERS:
                high, low = split(halved(f, value))
                both = mm(m.bph[f], high)
                m.hs[k, f] = both[:MODES] + both[MODES:] + mm(m.bph[f, 0:MODES, :], low)
                send(m.hs.at[k, f], m.hr.at[k, f ^ 1], m.hss.at[k, f], m.hrs.at[k, f ^ 1], beside[f])
        if k + 1 < ITERS:
            send_faces(k)
        else:
            send_faces(k)
        def dots(i, total, z=z, t=t, k=k):
            at = pl.ds(pl.multiple_of(i * CHUNK, CHUNK), CHUNK)
            low_at = pl.ds(pl.multiple_of(FACE_ROWS + i * CHUNK, CHUNK), CHUNK)
            return total + fold(m.inner[at, :] * (m.ts[k, at, :] + t[at, :])) + fold(z[low_at, :] * t[low_at, :])
        second = lax.fori_loop(0, FACE_ROWS // CHUNK, dots, zero)
        m.own[k, 1:2, :] = jnp.sum(second, axis=0, keepdims=True)
        if k + 1 < ITERS:
            m.cd[k, c] = m.own[k]
            for step in range(1, nc):
                mine = m.cd.at[k, c]
                send(mine, mine, m.css.at[k, step], m.crs.at[k, step], c_peer(step))
        else:
            m.fd[c, xm] = m.own[k]
            for dc, dx in wide:
                mine = m.fd.at[c, xm]
                send(mine, mine, m.fss.at[dc, dx], m.frs.at[dc, dx], cx_peer((dc, dx)))
        for at in inside_parts:
            value = t[at, :] + product(at, near)
            t[at, :] = value
            if k + 1 < ITERS:
                keep_halves(at, value)

        if k + 1 < ITERS:
            for at in near_parts:
                keep_halves(at, m.ts[k, at, :])
            part = coarse(0, ORDER)
            for f in range(4):
                slot = m.hr.at[k, f]
                remote(slot, slot, m.hss.at[k, f], m.hrs.at[k, f], beside[f]).wait_recv()
                part = part + m.hr[k, f]
            m.zg[k + 1, zm] = part
            z_gather_start(k + 1)
            for step in range(1, nc):
                slot = m.cd.at[k, c_at(-step)]
                remote(slot, slot, m.css.at[k, step], m.crs.at[k, step], c_peer(step)).wait_recv()
            sums = m.cd[k, 0]
            for j in range(1, nc):
                sums = sums + m.cd[k, j]
            z_sums(k + 1, sums)
            z_gather_forward(k + 1)
            coeff = coefficients(solve_coarse(k + 1), coeff)

    image_on_faces(ITERS - 1)
    for dc, dx in reversed(wide):
        slot = m.fd.at[c_at(-dc), x_at(-dx)]
        remote(slot, slot, m.fss.at[dc, dx], m.frs.at[dc, dx], cx_peer((dc, dx))).wait_recv()
    sums = m.fd[0, 0]
    for i in range(nc):
        for j in range(nx):
            if i or j:
                sums = sums + m.fd[i, j]
    z_sums(0, sums)
    sums = z_sums_total(0)
    _, ratio, alpha = coefficients(sums, coeff)
    z = m.z.at[ITERS - 1]
    t = m.t.at[ITERS - 1]

    def finish(at):
        m.out[0, at, :] = m.x[at, :] + alpha * (z[at, :] + ratio * m.d[at, :])
        m.out[1, at, :] = m.r[at, :] - alpha * (t[at, :] + ratio * m.s[at, :])
    half = ORDER // 2
    outs = []
    for i in range(2):
        loop_rows(i * half, half, finish)
        at = pl.ds(i * half, half)
        for j, into in enumerate((x_out, r_out)):
            outs.append(pltpu.make_async_copy(m.out.at[j, at, :], into.at[0, 0, at, :], m.lsem.at[2 * i + j]))
            outs[-1].start()
    for copy in outs:
        copy.wait()
    for copy in pending:
        copy.wait_send()


class Names:
    def __init__(self, names, refs):
        for name, ref in zip(names, refs, strict=True):
            setattr(self, name, ref)


def scratch(nx, nz, nc, width):
    vmem, dma = pltpu.VMEM, pltpu.SemaphoreType.DMA
    span = nz * MODES
    full, face = (ORDER, width), (FACE_ROWS, width)
    return dict(
        raw=vmem(full, F32), braw=vmem((MODES, ORDER), F32), mraw=vmem((MODES, nx * span), F32), craw=vmem((ORDER, ORDER), F32),
        fbs=pltpu.SMEM((4, nx * nz), jnp.int32), ers=pltpu.SMEM((2, 2, nx * nz), jnp.int32),
        chi=vmem((ORDER, ORDER), BF16), clo=vmem((ORDER, ORDER), BF16), vhi=vmem(full, BF16), vlo=vmem(full, BF16),
        bhl=vmem((2 * MODES, ORDER), BF16), bt=vmem((ORDER, BLOCK), BF16), bpt=vmem((FACE_ROWS, BLOCK), BF16), bph=vmem((4, 2 * MODES, BLOCK), BF16),
        hs=vmem((ITERS, 4, MODES, width), F32), hr=vmem((ITERS, 4, MODES, width), F32), hss=dma((ITERS, 4)), hrs=dma((ITERS, 4)),
        yk=vmem((5, BLOCK, width), BF16), mt=vmem((nx, MODES, span), F32), mhl=vmem((2 * nx * MODES, span), BF16),
        zg=vmem((ITERS, nz, MODES, width), F32), xs=vmem((ITERS, nx, PACK, width), F32), xr=vmem((ITERS, nx, PACK, width), F32),
        yo=vmem((ITERS, MODES, width), F32), yp=vmem((ITERS, 4, MODES, width), F32),
        ts=vmem((ITERS, *face), F32), tp=vmem((ITERS, *face), F32), cd=vmem((ITERS, nc, SUMS, width), F32),
        own=vmem((ITERS, SUMS, width), F32), dz=vmem((ITERS, nz, SUMS, width), F32), fd=vmem((nc, nx, SUMS, width), F32),
        bfs=vmem((4, MODES, BLOCK), F32), bfr=vmem((4, MODES, BLOCK), F32), rp=vmem(face, F32),
        z=vmem((ITERS, *full), F32), t=vmem((ITERS, *full), F32), q=vmem(full, F32), s=vmem(full, F32), r=vmem(full, F32),
        d=vmem(full, F32), x=vmem(full, F32), zp=vmem(face, F32), qp=vmem(face, F32), wp=vmem(face, F32), inner=vmem(face, F32), weight=vmem(face, F32), out=vmem((2, *full), F32),
        lsem=dma((8,)), zss=dma((ITERS, nz + 1)), zrs=dma((ITERS, nz + 1)), xss=dma((ITERS, nx)), xrs=dma((ITERS, nx)),
        yss=dma((ITERS, 4)), yrs=dma((ITERS, 4)), tss=dma((ITERS, 4)), trs=dma((ITERS, 4)), css=dma((ITERS, nc)), crs=dma((ITERS, nc)),
        dzs=dma((ITERS, nz)), dzr=dma((ITERS, nz)), fss=dma((nc, nx)), frs=dma((nc, nx)), mss=dma((nx,)), mrs=dma((nx,)),
        bss=dma((4,)), brs=dma((4,)), rss=dma((4,)), rrs=dma((4,)),
    )


def back_in_place(place_in, x, r, x_out, r_out, held, place, get, put, place_sem):
    pairs = [(p, j) for p in range(NBLOCKS) for j in range(2)]
    sources, intos = (x, r), (x_out, r_out)

    def load(p, j):
        at = pl.ds(p * BLOCK, BLOCK)
        return pltpu.make_async_copy(sources[j].at[0, 0, at, :], held.at[j, at, :], get.at[j, p])

    def store(p, j):
        at = pl.ds(pl.multiple_of(place[p] * BLOCK, BLOCK), BLOCK)
        return pltpu.make_async_copy(held.at[j, pl.ds(p * BLOCK, BLOCK), :], intos[j].at[0, 0, at, :], put.at[j, p])

    get_place = pltpu.make_async_copy(place_in, place, place_sem)
    get_place.start()
    for p, j in pairs:
        load(p, j).start()
    get_place.wait()
    for p, j in pairs:
        load(p, j).wait()
        store(p, j).start()
    for p, j in pairs:
        store(p, j).wait()


def shards(nx, nz, nc, compliance, loads, modes, coarse_inverse, face_block, edge_rows):
    width = loads.shape[-1]
    held = scratch(nx, nz, nc, width)

    def body(*refs):
        kernel(nx, nz, nc, *refs[:9], Names(held, refs[9:]))

    anywhere = pl.BlockSpec(memory_space=pl.ANY)
    small = pl.BlockSpec(memory_space=pltpu.SMEM)
    shapes = [jax.ShapeDtypeStruct(loads.shape, F32)] * 2
    x, r, place = pl.pallas_call(
        body,
        out_shape=shapes + [jax.ShapeDtypeStruct((NBLOCKS,), jnp.int32)],
        in_specs=[anywhere] * 6,
        out_specs=[anywhere, anywhere, small],
        scratch_shapes=list(held.values()),
        compiler_params=pltpu.CompilerParams(collective_id=0, has_side_effects=True, vmem_limit_bytes=56 * 1024 * 1024),
    )(compliance, loads, modes, coarse_inverse, jnp.transpose(face_block, (0, 2, 1)), jnp.transpose(edge_rows, (0, 2, 1)))
    return pl.pallas_call(
        back_in_place,
        out_shape=shapes,
        in_specs=[anywhere] * 3,
        out_specs=[anywhere, anywhere],
        scratch_shapes=[
            pltpu.VMEM((2, ORDER, width), F32), pltpu.SMEM((NBLOCKS,), jnp.int32),
            pltpu.SemaphoreType.DMA((2, NBLOCKS)), pltpu.SemaphoreType.DMA((2, NBLOCKS)), pltpu.SemaphoreType.DMA,
        ],
    )(place, x, r)


def solution(mesh, nz=NZ):
    nc, ns = mesh.shape["cluster"], mesh.shape["sub"]
    cut = P("cluster", "sub", None, None)
    return jax.shard_map(
        functools.partial(shards, ns // nz, nz, nc), mesh=mesh,
        in_specs=(cut, cut, cut, P("cluster", "sub", None), P(), P()),
        out_specs=(cut, cut), check_vma=False,
    )
```
